256 devices in a mesh: role: 4 (over x_lo, core), rep: 8 (over y, x_hi), tp: 8 (over z).
Axes of the slice: x: 4 (x_hi: 2, x_lo: 2; x = x_hi * 2 + x_lo), y: 4, z: 8, core: 2. Of those that a mesh axis runs over, the one named last changes fastest.
Arguments:
- master: float32 [16384, 1024], P(('tp', 'role', 'rep')), may hold values from -6 to 6
- moment: float32 [16384, 1024], P(('tp', 'role', 'rep')), may hold values from -6 to 6
- second: float32 [16384, 1024], P(('tp', 'role', 'rep')), may hold values from 0.25 to 4
- gradient: float32 [16384, 1024], P(('tp', 'role', 'rep')), may hold values from -6 to 6
- step_count: int32 [1], replicated, may hold values from 1 to 8
- old_weights: bfloat16 [16384, 1024], P('tp'), may hold values from -0.046875 to 0.046875
- branch_rows: bfloat16 [16384, 16384], P(('role', 'rep'), 'tp'), may hold values from -6 to 6
- assignment: int32 [16384, 1], P(('role', 'rep')), may hold values from 0 to 31; in each aligned block of 512 rows (0 to 511, 512 to 1023, ...) at most 32 rows name the same one
Outputs:
- new_master: float32 [16384, 1024], P(('tp', 'role', 'rep'))
- new_moment: float32 [16384, 1024], P(('tp', 'role', 'rep'))
- new_second: float32 [16384, 1024], P(('tp', 'role', 'rep'))
- rollout_weights: bfloat16 [16384, 1024], P('tp')
- branch_keys: bfloat16 [32, 32, 32, 1024], P(('role', 'rep'), None, None, 'tp')
The draws below stay inside these ranges and needn't reach their ends.
Inputs may be any that keep to these rules, and one draw needn't show every extreme that they name: `assignment`: in each aligned block of 512 rows (the rows that start on one replica) no replica is named by more than 32 rows; some replica is named by exactly 32 rows of some block.
All inputs are finite; a program needn't handle non-finite values.
Results may differ from the reference program's by a relative error of at most 0.001.
Values may be sent and summed in bfloat16 or wider, within the bound.
No kernel may reach another device: no remote copies, remote signals or barrier semaphores. Data moves between devices by JAX's collectives and lax.ppermute only.
A program may use at most 64 MiB of HBM per device.

```python
import math
import jax
import jax.numpy as jnp
import numpy as np
from jax import lax

D = 16384
HK = 1024
ROWS_REP = 512
CAP = 32
ROWS = 16384
N_ROLE = 4
N_REP = 8


def shard_levels(rng, extent, pieces, smallest, top_value):
    factor_of = 1.0
    for axis_at, parts in pieces:
        draws = jax.random.uniform(jax.random.fold_in(jax.random.fold_in(rng, 6), axis_at), (parts,), jnp.float32, smallest / len(pieces), top_value / len(pieces))
        factor_of = factor_of * jnp.repeat(jnp.exp(draws), extent[axis_at] // parts).reshape((-1,) + (1,) * (len(extent) - 1 - axis_at))
    return factor_of


def shared_out(rng, own, number, rows, number_of, top, most, skew):
    sequence = jax.random.permutation(rng, number_of)
    heavy_load, usual = shares(number_of, rows * top, most, skew, True), shares(number_of, rows * top, most, skew, False)
    places = jnp.arange(number_of)

    def named(tallies, rotation):
        used = int((tallies > 0).sum())
        fixed = max(1, used // 4)
        shifted = fixed + (places - fixed + rotation * (used - fixed)) % max(1, number_of - fixed)
        return jnp.zeros((number_of,), jnp.int32).at[sequence[jnp.where(places < fixed, places, shifted)]].set(jnp.asarray(tallies, jnp.int32))

    tallies = jnp.where(number % 4 == 0, named(heavy_load, number // 4), named(usual, number - number // 4 - 1))
    mixed = jax.random.permutation(jax.random.fold_in(own, 3), number_of)
    giver, taker = mixed[0:number_of // 2 * 2:2], mixed[1:number_of // 2 * 2:2]
    margin = jnp.minimum(tallies[giver] - 1, most - tallies[taker]) // 2
    margin = jnp.where((giver == sequence[0]) | (taker == sequence[0]) | (tallies[taker] == 0), 0, jnp.maximum(margin, 0))
    shifted = jax.random.randint(jax.random.fold_in(own, 4), (number_of // 2,), 0, 1 << 20) % (margin + 1)
    tallies = tallies.at[giver].add(-shifted).at[taker].add(shifted)
    items = jnp.searchsorted(jnp.cumsum(tallies), jnp.arange(rows * top), side="right").astype(jnp.int32)
    grid = items.reshape(top, rows).T
    grid = grid[jax.random.permutation(jax.random.fold_in(own, 1), rows)]
    rotation = jax.random.randint(jax.random.fold_in(own, 2), (rows, 1), 0, top)
    return jnp.take_along_axis(grid, (jnp.arange(top)[None, :] + rotation) % top, axis=1)


def shares(amount, total, most, slope, full):
    weights = [(1 << 20) // math.isqrt(standing ** slope) + 1 for standing in range(1, amount + 1)]
    largest = most if full else min(most, max(-(-total // amount), total * weights[0] // sum(weights)))
    least = 1 if total - largest >= amount - 1 else 0
    given, surplus = [largest] + [least] * (amount - 1), total - largest - least * (amount - 1)
    while surplus > 0:
        movable = [i for i in range(1, amount) if given[i] < largest] or [i for i in range(1, amount) if given[i] < most]
        mass, remaining = sum([weights[i] for i in movable]), surplus
        for i in movable:
            addition = min(most - given[i], max(1, remaining * weights[i] // mass), surplus)
            given[i] = given[i] + addition
            surplus = surplus - addition
    return np.array(given)


def centred(rng, dims, deviation, reach, split=(), kind=jnp.bfloat16):
    gain = shard_levels(rng, dims, split, -0.22, 0.18) if split else 1.0
    entries = jax.random.normal(rng, dims, jnp.float32) * deviation * gain
    return jnp.minimum(jnp.maximum(entries, -reach), reach).astype(kind)


def setup_inputs(seed: int = 0) -> dict:
    key_of = jax.random.split(jax.random.key(seed), 9)
    master = centred(key_of[0], (D, HK), 1.0, 6.0, ((0, 256),), jnp.float32)
    moment = centred(key_of[1], (D, HK), 1.0, 6.0, ((0, 256),), jnp.float32)
    second = jnp.clip(jnp.exp(math.log(4.0) - 2.7725887 * jax.random.uniform(key_of[2], (D, HK), jnp.float32) ** shard_levels(key_of[2], (D, HK), ((0, 256),), -0.2, 0.2)), 0.25, 4.0)
    gradient = centred(key_of[3], (D, HK), 1.0, 6.0, ((0, 256),), jnp.float32)
    step_count = jax.random.randint(key_of[4], (1,), 1, 9).astype(jnp.int32)
    old_weights = centred(key_of[5], (D, HK), D ** -0.5, 0.046875, ((0, 8),))
    branch_rows = centred(key_of[6], (ROWS, D), 1.0, 6.0, ((0, 32), (1, 8)))
    assignment_keys = jax.random.split(jax.random.fold_in(key_of[7], 1), ROWS // ROWS_REP)
    assignment_turns = jax.random.permutation(jax.random.fold_in(key_of[7], 3), ROWS // ROWS_REP)
    assignment = jax.vmap(lambda own, number: shared_out(jax.random.fold_in(key_of[7], 2), own, number, ROWS_REP, N_ROLE * N_REP, 1, CAP, 1))(assignment_keys, assignment_turns).reshape((ROWS, 1))
    return {"master": master, "moment": moment, "second": second, "gradient": gradient, "step_count": step_count, "old_weights": old_weights, "branch_rows": branch_rows, "assignment": assignment}


learn_rate = 0.05
decay_rate = 0.1

def reference(master, moment, second, gradient, step_count, old_weights, branch_rows, assignment):
    steps_f = step_count[0].astype(jnp.float32)
    first_fix = 1.0 - jnp.power(jnp.float32(0.9), steps_f)
    second_fix = 1.0 - jnp.power(jnp.float32(0.95), steps_f)
    new_moment = 0.9 * moment + 0.1 * gradient
    new_second = 0.95 * second + 0.05 * gradient * gradient
    update = new_moment / first_fix / (jnp.sqrt(new_second / second_fix) + 1e-08)
    new_master = master - learn_rate * (update + decay_rate * master)
    rollout_weights = new_master.astype(jnp.bfloat16)
    keys = jnp.dot(branch_rows, old_weights, preferred_element_type=jnp.float32).astype(jnp.bfloat16)
    replicas = N_ROLE * N_REP
    target = assignment[:, 0].astype(jnp.int32)
    onehot = (target.reshape(replicas, ROWS_REP)[:, :, None] == jnp.arange(replicas, dtype=jnp.int32)[None, None, :]).astype(jnp.int32)
    ranks = lax.optimization_barrier(jnp.sum((jnp.cumsum(onehot, axis=1) - 1) * onehot, axis=2)).reshape(-1).astype(jnp.int32)
    source = (jnp.arange(replicas * ROWS_REP, dtype=jnp.int32) // ROWS_REP).astype(jnp.int32)
    branch_keys = jnp.zeros((replicas, replicas, CAP, HK), jnp.bfloat16).at[target, source, ranks].set(keys)
    return (new_master, new_moment, new_second, rollout_weights, branch_keys)
```

```python
import jax
import jax.numpy as jnp
from jax import lax
from jax.sharding import PartitionSpec as P

learn_rate = 0.05
decay_rate = 0.1


def slot_matrix(assignment, replicas, slots_each):
    target = assignment[:, 0]
    targets = jnp.arange(replicas, dtype=jnp.int32)
    onehot = (target[:, None] == targets[None, :]).astype(jnp.int32)
    ranks = jnp.sum((jnp.cumsum(onehot, axis=0) - 1) * onehot, axis=1)
    position = target * slots_each + ranks
    places = jnp.arange(replicas * slots_each, dtype=jnp.int32)
    return (places[:, None] == position[None, :]).astype(jnp.bfloat16)


def local(master, moment, second, gradient, step_count, old_weights, branch_rows, assignment):
    steps_f = step_count[0].astype(jnp.float32)
    first_fix = 1.0 - jnp.power(jnp.float32(0.9), steps_f)
    second_fix = 1.0 - jnp.power(jnp.float32(0.95), steps_f)
    new_moment = 0.9 * moment + 0.1 * gradient
    new_second = 0.95 * second + 0.05 * gradient * gradient
    update = new_moment / first_fix / (jnp.sqrt(new_second / second_fix) + 1e-08)
    new_master = master - learn_rate * (update + decay_rate * master)
    rollout_weights = lax.all_gather(
        new_master.astype(jnp.bfloat16), ("role", "rep"), axis=0, tiled=True
    )
    replicas = lax.axis_size(("role", "rep"))
    rows_here = branch_rows.shape[0]
    slots_each = 2 * rows_here // replicas
    selector = slot_matrix(assignment, replicas, slots_each)
    partial_value = jnp.dot(branch_rows, old_weights, preferred_element_type=jnp.float32)
    keys = lax.psum_scatter(partial_value, "tp", scatter_dimension=1, tiled=True).astype(jnp.bfloat16)
    placed = jnp.dot(selector, keys, preferred_element_type=jnp.float32).astype(jnp.bfloat16)
    placed = placed.reshape(replicas, slots_each, keys.shape[1])
    arrived = lax.all_to_all(placed, ("role", "rep"), split_axis=0, concat_axis=0, tiled=True)
    branch_keys = arrived.reshape(1, replicas, slots_each, keys.shape[1])
    return (new_master, new_moment, new_second, rollout_weights, branch_keys)


def solution(mesh):
    placed = (
        P(("tp", "role", "rep"), None),
        P(("tp", "role", "rep"), None),
        P(("tp", "role", "rep"), None),
        P(("tp", "role", "rep"), None),
        P(),
        P("tp", None),
        P(("role", "rep"), "tp"),
        P(("role", "rep"), None),
    )
    return jax.shard_map(
        local,
        mesh=mesh,
        in_specs=placed,
        out_specs=(
            P(("tp", "role", "rep"), None),
            P(("tp", "role", "rep"), None),
            P(("tp", "role", "rep"), None),
            P("tp", None),
            P(("role", "rep"), None, None, "tp"),
        ),
        check_vma=False,
    )
```

```python
import functools

import jax
import jax.numpy as jnp
from jax import lax
from jax.experimental import pallas as pl
from jax.experimental.pallas import tpu as pltpu
from jax.sharding import Mesh
from jax.sharding import PartitionSpec as P

learn_rate = 0.05
decay_rate = 0.1

PLANE = ("xlo", "core", "y", "xhi")
CHIPS = ("xlo", "y", "xhi")
LEVELS = 32767.0
TAIL = 16


def coded(value):
    top = jnp.maximum(jnp.max(jnp.abs(value), axis=0, keepdims=True), 1.2e-38)
    power = jnp.ceil(jnp.log(top) * (256.0 / 0.6931471805599453) + 0.01)
    power = jnp.clip(power, -32256.0, 32256.0)
    scaled = value * jnp.exp2(power * (-1.0 / 256.0)) * LEVELS
    codes = jnp.clip(jnp.round(scaled), -LEVELS, LEVELS)
    tail = jnp.broadcast_to(power, (TAIL, value.shape[1]))
    return codes.astype(jnp.int32).astype(jnp.int16), tail.astype(jnp.int32).astype(jnp.int16)


def put_coded(ref, value):
    codes, tail = coded(value)
    rows = value.shape[0]
    ref[0:rows, :] = codes
    ref[rows : rows + TAIL, :] = tail


def take_coded(ref):
    rows = ref.shape[0] - TAIL
    power = ref[rows : rows + TAIL, :].astype(jnp.int32).astype(jnp.float32)[0:1, :]
    codes = ref[0:rows, :].astype(jnp.int32).astype(jnp.float32)
    return codes * (1.0 / LEVELS) * jnp.exp2(power * (1.0 / 256.0))


def product(rows_ref, columns_ref):
    return jnp.dot(rows_ref[...], columns_ref[...], preferred_element_type=jnp.float32)


def far_kernel(ids, x, wa, wb, wc, qa, qb, qc, qd):
    half = x.shape[0] // 2
    put_coded(qa, product(x, wa))
    put_coded(qb, product(x, wb))
    far = product(x, wc)
    put_coded(qc, far[:half])
    put_coded(qd, far[half:])


def near_kernel(ids, x, wa, wb, wc, wd, we, qa, qb, pc, pd, pe):
    put_coded(qa, product(x, wa))
    put_coded(qb, product(x, wb))
    pc[...] = product(x, wc)
    pd[...] = product(x, wd)
    pe[...] = product(x, we)


def products(kernel, x, w, ids, count, width, outs):
    rows, depth = x.shape
    whole = lambda g, ids: (0, 0)
    columns = [
        pl.BlockSpec((depth, width), functools.partial(lambda k, g, ids: (0, ids[k]), k))
        for k in range(count)
    ]
    return pl.pallas_call(
        kernel,
        out_shape=outs,
        grid_spec=pltpu.PrefetchScalarGridSpec(
            num_scalar_prefetch=1,
            grid=(1,),
            in_specs=[pl.BlockSpec((rows, depth), whole)] + columns,
            out_specs=[pl.BlockSpec(o.shape, whole) for o in outs],
        ),
        compiler_params=pltpu.CompilerParams(vmem_limit_bytes=40 * 2**20),
        cost_estimate=pl.CostEstimate(
            flops=2 * rows * depth * width * count,
            bytes_accessed=2 * depth * (rows + width * count),
            transcendentals=0,
        ),
    )(ids, x, *([w] * count))


def local_call(kernel, outs, *args, flops=0):
    return pl.pallas_call(
        kernel,
        out_shape=outs,
        compiler_params=pltpu.CompilerParams(vmem_limit_bytes=40 * 2**20),
        cost_estimate=pl.CostEstimate(flops=flops, bytes_accessed=2**20, transcendentals=0),
    )(*args)


def merge_kernel(own_a, next_a, far_a, own_b, next_b, far_b, qa, qb):
    half = own_a.shape[0] // 2
    total = own_a[...] + take_coded(next_a)
    total = jnp.concatenate([total[:half] + take_coded(far_a), total[half:]], axis=0)
    put_coded(qa, total)
    total = own_b[...] + take_coded(next_b)
    total = jnp.concatenate([total[:half], total[half:] + take_coded(far_b)], axis=0)
    put_coded(qb, total)


def selector_kernel(target_ref, out):
    places, rows = out.shape
    replicas = 32
    each = places // replicas
    target = target_ref[...]
    onehot = (lax.broadcasted_iota(jnp.int32, (replicas, rows), 0) == target).astype(jnp.float32)
    before = (
        lax.broadcasted_iota(jnp.int32, (rows, rows), 0)
        < lax.broadcasted_iota(jnp.int32, (rows, rows), 1)
    ).astype(jnp.bfloat16)
    ranks = jnp.dot(onehot.astype(jnp.bfloat16), before, preferred_element_type=jnp.float32)
    rank = jnp.sum(ranks * onehot, axis=0, keepdims=True).astype(jnp.int32)
    position = target * each + rank
    out[...] = (lax.broadcasted_iota(jnp.int32, (places, rows), 0) == position).astype(jnp.float32).astype(jnp.bfloat16)


def final_kernel(own, ra, rb, rc, rd, selector, out):
    keys = own[...] + take_coded(ra) + take_coded(rb) + take_coded(rc) + take_coded(rd)
    out[...] = jnp.dot(
        selector[...], keys.astype(jnp.bfloat16), preferred_element_type=jnp.float32
    ).astype(jnp.bfloat16)


def along_tp(value, step):
    size = lax.axis_size("tp")
    return lax.ppermute(value, "tp", [(i, (i + step) % size) for i in range(size)])


def local(master, moment, second, gradient, step_count, old_weights, branch_rows, assignment):
    steps_f = step_count[0].astype(jnp.float32)
    first_fix = 1.0 - jnp.power(jnp.float32(0.9), steps_f)
    second_fix = 1.0 - jnp.power(jnp.float32(0.95), steps_f)
    new_moment = 0.9 * moment + 0.1 * gradient
    new_second = 0.95 * second + 0.05 * gradient * gradient
    update = new_moment / first_fix / (jnp.sqrt(new_second / second_fix) + 1e-08)
    new_master = master - learn_rate * (update + decay_rate * master)

    rows, width = new_master.shape
    chips = lax.axis_size(CHIPS)
    fresh = new_master.astype(jnp.bfloat16)
    spread = jnp.broadcast_to(fresh[None], (chips, rows, width))
    mine = lax.all_to_all(spread, CHIPS, split_axis=0, concat_axis=0, tiled=True)
    other = lax.ppermute(mine, "core", [(0, 1), (1, 0)])
    core = lax.axis_index("core")
    pair = jnp.stack([jnp.where(core == 0, mine, other), jnp.where(core == 0, other, mine)])
    pair = pair.reshape(2, lax.axis_size("xlo"), -1, width)
    rollout_weights = jnp.swapaxes(pair, 0, 1).reshape(2 * chips * rows, width)

    size = lax.axis_size("tp")
    me = lax.axis_index("tp")
    count = branch_rows.shape[0]
    part = old_weights.shape[1] // size
    code = lambda n: jax.ShapeDtypeStruct((n + TAIL, part), jnp.int16)
    full = jax.ShapeDtypeStruct((count, part), jnp.float32)
    ids = lax.rem(me + jnp.array([3, 5, 4], jnp.int32), size)
    q3, q5, q4a, q4b = products(
        far_kernel, branch_rows, old_weights, ids, 3, part,
        [code(count), code(count), code(count // 2), code(count // 2)],
    )
    r3, r5 = along_tp(q3, 1), along_tp(q5, -1)
    r4a, r4b = along_tp(q4a, 2), along_tp(q4b, -2)
    ids = lax.rem(me + jnp.array([1, 7, 2, 6, 0], jnp.int32), size)
    q1, q7, p2, p6, p0 = products(
        near_kernel, branch_rows, old_weights, ids, 5, part,
        [code(count), code(count), full, full, full],
    )
    r1, r7 = along_tp(q1, 1), along_tp(q7, -1)
    q2, q6 = local_call(merge_kernel, [code(count), code(count)], p2, r3, r4a, p6, r5, r4b)
    r2, r6 = along_tp(q2, 2), along_tp(q6, -2)
    replicas = lax.axis_size(PLANE)
    slots_each = 2 * count // replicas
    places = replicas * slots_each
    selector = local_call(
        selector_kernel, jax.ShapeDtypeStruct((places, count), jnp.bfloat16), assignment.reshape(1, count)
    )
    placed = local_call(
        final_kernel, jax.ShapeDtypeStruct((places, part), jnp.bfloat16), p0, r1, r7, r2, r6, selector
    )
    placed = placed.reshape(replicas, slots_each, part)
    arrived = lax.all_to_all(placed, PLANE, split_axis=0, concat_axis=0, tiled=True)
    branch_keys = arrived.reshape(1, replicas, slots_each, part)
    return (new_master, new_moment, new_second, rollout_weights, branch_keys)


def solution(mesh):
    size = mesh.shape
    mesh = Mesh(
        mesh.devices.reshape(2, 2, 4, 2, size["tp"]), ("xlo", "core", "y", "xhi", "tp")
    )
    shard = P(("tp",) + PLANE, None)
    return jax.shard_map(
        local,
        mesh=mesh,
        in_specs=(shard, shard, shard, shard, P(), P("tp", None), P(PLANE, "tp"), P(PLANE, None)),
        out_specs=(shard, shard, shard, P("tp", None), P(PLANE, None, None, "tp")),
        check_vma=False,
    )
```

```python
import functools

import jax
import jax.numpy as jnp
from jax import lax
from jax.experimental import pallas as pl
from jax.experimental.pallas import tpu as pltpu
from jax.sharding import Mesh
from jax.sharding import PartitionSpec as P

learn_rate = 0.05
decay_rate = 0.1

PLANE = ("xlo", "core", "y", "xhi")
CHIPS = ("xlo", "y", "xhi")
LEVELS = 32767.0
TAIL = 16


def coded(value):
    top = jnp.maximum(jnp.max(jnp.abs(value), axis=0, keepdims=True), 1.2e-38)
    power = jnp.ceil(jnp.log(top) * (256.0 / 0.6931471805599453) + 0.01)
    power = jnp.clip(power, -32256.0, 32256.0)
    scaled = value * jnp.exp2(power * (-1.0 / 256.0)) * LEVELS
    codes = jnp.clip(jnp.round(scaled), -LEVELS, LEVELS)
    tail = jnp.broadcast_to(power, (TAIL, value.shape[1]))
    return codes.astype(jnp.int32).astype(jnp.int16), tail.astype(jnp.int32).astype(jnp.int16)


def put_coded(ref, value):
    codes, tail = coded(value)
    rows = value.shape[0]
    ref[0:rows, :] = codes
    ref[rows : rows + TAIL, :] = tail


def take_coded(ref):
    rows = ref.shape[0] - TAIL
    power = ref[rows : rows + TAIL, :].astype(jnp.int32).astype(jnp.float32)[0:1, :]
    codes = ref[0:rows, :].astype(jnp.int32).astype(jnp.float32)
    return codes * (1.0 / LEVELS) * jnp.exp2(power * (1.0 / 256.0))


def product(rows_ref, columns_ref):
    return jnp.dot(rows_ref[...], columns_ref[...], preferred_element_type=jnp.float32)


def far_kernel(ids, x, wa, wb, wc, qa, qb, qc, qd):
    half = x.shape[0] // 2
    put_coded(qa, product(x, wa))
    put_coded(qb, product(x, wb))
    far = product(x, wc)
    put_coded(qc, far[:half])
    put_coded(qd, far[half:])


def near_kernel(ids, x, wa, wb, wc, wd, we, qa, qb, pc, pd, pe):
    put_coded(qa, product(x, wa))
    put_coded(qb, product(x, wb))
    pc[...] = product(x, wc)
    pd[...] = product(x, wd)
    pe[...] = product(x, we)


def products(kernel, x, w, ids, count, width, outs):
    rows, depth = x.shape
    whole = lambda g, ids: (0, 0)
    columns = [
        pl.BlockSpec((depth, width), functools.partial(lambda k, g, ids: (0, ids[k]), k))
        for k in range(count)
    ]
    return pl.pallas_call(
        kernel,
        out_shape=outs,
        grid_spec=pltpu.PrefetchScalarGridSpec(
            num_scalar_prefetch=1,
            grid=(1,),
            in_specs=[pl.BlockSpec((rows, depth), whole)] + columns,
            out_specs=[pl.BlockSpec(o.shape, whole) for o in outs],
        ),
        compiler_params=pltpu.CompilerParams(vmem_limit_bytes=40 * 2**20),
        cost_estimate=pl.CostEstimate(
            flops=2 * rows * depth * width * count,
            bytes_accessed=2 * depth * (rows + width * count),
            transcendentals=0,
        ),
    )(ids, x, *([w] * count))


def local_call(kernel, outs, *args, flops=0):
    return pl.pallas_call(
        kernel,
        out_shape=outs,
        compiler_params=pltpu.CompilerParams(vmem_limit_bytes=40 * 2**20),
        cost_estimate=pl.CostEstimate(flops=flops, bytes_accessed=2**20, transcendentals=0),
    )(*args)


def merge_kernel(own_a, next_a, far_a, own_b, next_b, far_b, qa, qb):
    half = own_a.shape[0] // 2
    total = own_a[...] + take_coded(next_a)
    total = jnp.concatenate([total[:half] + take_coded(far_a), total[half:]], axis=0)
    put_coded(qa, total)
    total = own_b[...] + take_coded(next_b)
    total = jnp.concatenate([total[:half], total[half:] + take_coded(far_b)], axis=0)
    put_coded(qb, total)


def selector_kernel(target_ref, out):
    places, rows = out.shape
    replicas = 32
    each = places // replicas
    target = target_ref[...]
    onehot = (lax.broadcasted_iota(jnp.int32, (replicas, rows), 0) == target).astype(jnp.float32)
    before = (
        lax.broadcasted_iota(jnp.int32, (rows, rows), 0)
        < lax.broadcasted_iota(jnp.int32, (rows, rows), 1)
    ).astype(jnp.bfloat16)
    ranks = jnp.dot(onehot.astype(jnp.bfloat16), before, preferred_element_type=jnp.float32)
    rank = jnp.sum(ranks * onehot, axis=0, keepdims=True).astype(jnp.int32)
    position = target * each + rank
    out[...] = (lax.broadcasted_iota(jnp.int32, (places, rows), 0) == position).astype(jnp.float32).astype(jnp.bfloat16)


def final_kernel(own, ra, rb, rc, rd, selector, out):
    keys = own[...] + take_coded(ra) + take_coded(rb) + take_coded(rc) + take_coded(rd)
    out[...] = jnp.dot(
        selector[...], keys.astype(jnp.bfloat16), preferred_element_type=jnp.float32
    ).astype(jnp.bfloat16)


def half_kernel(place, half, *refs):
    out, sems = refs[-2:]
    copies = [
        pltpu.make_async_copy(half.at[i], out.at[i, place[0]], sems.at[i])
        for i in range(half.shape[0])
    ]
    for copy in copies:
        copy.start()
    for copy in copies:
        copy.wait()


def set_half(place, half, pair=None):
    anywhere = pl.BlockSpec(memory_space=pl.ANY)
    lanes, rows, width = half.shape
    args = (place, half) + (() if pair is None else (pair,))
    return pl.pallas_call(
        half_kernel,
        out_shape=jax.ShapeDtypeStruct((lanes, 2, rows, width), half.dtype),
        in_specs=[pl.BlockSpec(memory_space=pltpu.SMEM)] + [anywhere] * (len(args) - 1),
        out_specs=anywhere,
        scratch_shapes=[pltpu.SemaphoreType.DMA((lanes,))],
        input_output_aliases={} if pair is None else {2: 0},
        cost_estimate=pl.CostEstimate(flops=0, bytes_accessed=2 * half.size * 2, transcendentals=0),
    )(*args)


def along_tp(value, step):
    size = lax.axis_size("tp")
    return lax.ppermute(value, "tp", [(i, (i + step) % size) for i in range(size)])


def local(master, moment, second, gradient, step_count, old_weights, branch_rows, assignment):
    steps_f = step_count[0].astype(jnp.float32)
    first_fix = 1.0 - jnp.power(jnp.float32(0.9), steps_f)
    second_fix = 1.0 - jnp.power(jnp.float32(0.95), steps_f)
    new_moment = 0.9 * moment + 0.1 * gradient
    new_second = 0.95 * second + 0.05 * gradient * gradient
    update = new_moment / first_fix / (jnp.sqrt(new_second / second_fix) + 1e-08)
    new_master = master - learn_rate * (update + decay_rate * master)

    rows, width = new_master.shape
    chips = lax.axis_size(CHIPS)
    fresh = new_master.astype(jnp.bfloat16)
    spread = jnp.broadcast_to(fresh[None], (chips, rows, width))
    mine = lax.all_to_all(spread, CHIPS, split_axis=0, concat_axis=0, tiled=True)
    size = lax.axis_size("tp")
    me = lax.axis_index("tp")
    count = branch_rows.shape[0]
    part = old_weights.shape[1] // size
    code = lambda n: jax.ShapeDtypeStruct((n + TAIL, part), jnp.int16)
    full = jax.ShapeDtypeStruct((count, part), jnp.float32)
    ids = lax.rem(me + jnp.array([3, 5, 4], jnp.int32), size)
    q3, q5, q4a, q4b = products(
        far_kernel, branch_rows, old_weights, ids, 3, part,
        [code(count), code(count), code(count // 2), code(count // 2)],
    )
    r3, r5 = along_tp(q3, 1), along_tp(q5, -1)
    r4a, r4b = along_tp(q4a, 2), along_tp(q4b, -2)
    ids = lax.rem(me + jnp.array([1, 7, 2, 6, 0], jnp.int32), size)
    q1, q7, p2, p6, p0 = products(
        near_kernel, branch_rows, old_weights, ids, 5, part,
        [code(count), code(count), full, full, full],
    )
    r1, r7 = along_tp(q1, 1), along_tp(q7, -1)
    q2, q6 = local_call(merge_kernel, [code(count), code(count)], p2, r3, r4a, p6, r5, r4b)
    r2, r6 = along_tp(q2, 2), along_tp(q6, -2)
    replicas = lax.axis_size(PLANE)
    slots_each = 2 * count // replicas
    places = replicas * slots_each
    selector = local_call(
        selector_kernel, jax.ShapeDtypeStruct((places, count), jnp.bfloat16), assignment.reshape(1, count)
    )
    placed = local_call(
        final_kernel, jax.ShapeDtypeStruct((places, part), jnp.bfloat16), p0, r1, r7, r2, r6, selector
    )
    placed, mine = lax.optimization_barrier((placed, mine))
    placed = placed.reshape(replicas, slots_each, part)
    arrived = lax.all_to_all(placed, PLANE, split_axis=0, concat_axis=0, tiled=True)
    branch_keys = arrived.reshape(1, replicas, slots_each, part)
    other = lax.ppermute(mine, "core", [(0, 1), (1, 0)])
    core = jnp.reshape(lax.axis_index("core"), (1,)).astype(jnp.int32)
    lanes = lax.axis_size("xlo")
    mine = mine.reshape(lanes, -1, width)
    other = other.reshape(lanes, -1, width)
    pair = set_half(core, mine)
    pair = set_half(1 - core, other, pair)
    rollout_weights = pair.reshape(2 * chips * rows, width)
    return (new_master, new_moment, new_second, rollout_weights, branch_keys)


def solution(mesh):
    size = mesh.shape
    mesh = Mesh(
        mesh.devices.reshape(2, 2, 4, 2, size["tp"]), ("xlo", "core", "y", "xhi", "tp")
    )
    shard = P(("tp",) + PLANE, None)
    return jax.shard_map(
        local,
        mesh=mesh,
        in_specs=(shard, shard, shard, shard, P(), P("tp", None), P(PLANE, "tp"), P(PLANE, None)),
        out_specs=(shard, shard, shard, P("tp", None), P(PLANE, None, None, "tp")),
        check_vma=False,
    )
```

```python
import functools

import jax
import jax.numpy as jnp
from jax import lax
from jax.experimental import pallas as pl
from jax.experimental.pallas import tpu as pltpu
from jax.sharding import Mesh
from jax.sharding import PartitionSpec as P

learn_rate = 0.05
decay_rate = 0.1

PLANE = ("xlo", "core", "y", "xhi")
CHIPS = ("xlo", "y", "xhi")
LEVELS = 32767.0
TAIL = 16


def coded(value):
    top = jnp.maximum(jnp.max(jnp.abs(value), axis=0, keepdims=True), 1.2e-38)
    power = jnp.ceil(jnp.log(top) * (256.0 / 0.6931471805599453) + 0.01)
    power = jnp.clip(power, -32256.0, 32256.0)
    scaled = value * jnp.exp2(power * (-1.0 / 256.0)) * LEVELS
    codes = jnp.clip(jnp.round(scaled), -LEVELS, LEVELS)
    tail = jnp.broadcast_to(power, (TAIL, value.shape[1]))
    return codes.astype(jnp.int32).astype(jnp.int16), tail.astype(jnp.int32).astype(jnp.int16)


def put_coded(ref, value):
    codes, tail = coded(value)
    rows = value.shape[0]
    ref[0:rows, :] = codes
    ref[rows : rows + TAIL, :] = tail


def take_coded(ref):
    rows = ref.shape[0] - TAIL
    power = ref[rows : rows + TAIL, :].astype(jnp.int32).astype(jnp.float32)[0:1, :]
    codes = ref[0:rows, :].astype(jnp.int32).astype(jnp.float32)
    return codes * (1.0 / LEVELS) * jnp.exp2(power * (1.0 / 256.0))


def product(rows_ref, columns_ref):
    return jnp.dot(rows_ref[...], columns_ref[...], preferred_element_type=jnp.float32)


def far_kernel(ids, x, wa, wb, wc, qa, qb, qc, qd):
    half = x.shape[0] // 2
    put_coded(qa, product(x, wa))
    put_coded(qb, product(x, wb))
    far = product(x, wc)
    put_coded(qc, far[:half])
    put_coded(qd, far[half:])


def near_kernel(ids, x, wa, wb, wc, wd, we, qa, qb, pc, pd, pe):
    put_coded(qa, product(x, wa))
    put_coded(qb, product(x, wb))
    pc[...] = product(x, wc)
    pd[...] = product(x, wd)
    pe[...] = product(x, we)


def products(kernel, x, w, ids, count, width, outs):
    rows, depth = x.shape
    whole = lambda g, ids: (0, 0)
    columns = [
        pl.BlockSpec((depth, width), functools.partial(lambda k, g, ids: (0, ids[k]), k))
        for k in range(count)
    ]
    return pl.pallas_call(
        kernel,
        out_shape=outs,
        grid_spec=pltpu.PrefetchScalarGridSpec(
            num_scalar_prefetch=1,
            grid=(1,),
            in_specs=[pl.BlockSpec((rows, depth), whole)] + columns,
            out_specs=[pl.BlockSpec(o.shape, whole) for o in outs],
        ),
        compiler_params=pltpu.CompilerParams(vmem_limit_bytes=40 * 2**20),
        cost_estimate=pl.CostEstimate(
            flops=2 * rows * depth * width * count,
            bytes_accessed=2 * depth * (rows + width * count),
            transcendentals=0,
        ),
    )(ids, x, *([w] * count))


def local_call(kernel, outs, *args, flops=0):
    return pl.pallas_call(
        kernel,
        out_shape=outs,
        compiler_params=pltpu.CompilerParams(vmem_limit_bytes=40 * 2**20),
        cost_estimate=pl.CostEstimate(flops=flops, bytes_accessed=2**20, transcendentals=0),
    )(*args)


def merge_kernel(own_a, next_a, far_a, own_b, next_b, far_b, qa, qb):
    half = own_a.shape[0] // 2
    total = own_a[...] + take_coded(next_a)
    total = jnp.concatenate([total[:half] + take_coded(far_a), total[half:]], axis=0)
    put_coded(qa, total)
    total = own_b[...] + take_coded(next_b)
    total = jnp.concatenate([total[:half], total[half:] + take_coded(far_b)], axis=0)
    put_coded(qb, total)


def selector_kernel(target_ref, out):
    places, rows = out.shape
    replicas = 32
    each = places // replicas
    target = target_ref[...]
    onehot = (lax.broadcasted_iota(jnp.int32, (replicas, rows), 0) == target).astype(jnp.float32)
    before = (
        lax.broadcasted_iota(jnp.int32, (rows, rows), 0)
        < lax.broadcasted_iota(jnp.int32, (rows, rows), 1)
    ).astype(jnp.bfloat16)
    ranks = jnp.dot(onehot.astype(jnp.bfloat16), before, preferred_element_type=jnp.float32)
    rank = jnp.sum(ranks * onehot, axis=0, keepdims=True).astype(jnp.int32)
    position = target * each + rank
    out[...] = (lax.broadcasted_iota(jnp.int32, (places, rows), 0) == position).astype(jnp.float32).astype(jnp.bfloat16)


def final_kernel(own, ra, rb, rc, rd, selector, out):
    keys = own[...] + take_coded(ra) + take_coded(rb) + take_coded(rc) + take_coded(rd)
    out[...] = jnp.dot(
        selector[...], keys.astype(jnp.bfloat16), preferred_element_type=jnp.float32
    ).astype(jnp.bfloat16)


def half_kernel(place, half, *refs):
    refs[-1][...] = half[...].reshape(refs[-1].shape)


def set_half(place, half, pair=None):
    lanes, rows, width = half.shape
    step = rows // 2
    args = (place, half) + (() if pair is None else (pair,))
    return pl.pallas_call(
        half_kernel,
        out_shape=jax.ShapeDtypeStruct((lanes, 2, rows, width), half.dtype),
        grid_spec=pltpu.PrefetchScalarGridSpec(
            num_scalar_prefetch=1,
            grid=(lanes, rows // step),
            in_specs=[pl.BlockSpec((1, step, width), lambda i, j, place: (i, j, 0))]
            + [pl.BlockSpec(memory_space=pl.ANY)] * (len(args) - 2),
            out_specs=pl.BlockSpec((1, 1, step, width), lambda i, j, place: (i, place[0], j, 0)),
        ),
        input_output_aliases={} if pair is None else {2: 0},
        compiler_params=pltpu.CompilerParams(vmem_limit_bytes=16 * 2**20),
        cost_estimate=pl.CostEstimate(flops=0, bytes_accessed=4 * half.size, transcendentals=0),
    )(*args)


def along_tp(value, step):
    size = lax.axis_size("tp")
    return lax.ppermute(value, "tp", [(i, (i + step) % size) for i in range(size)])


def local(master, moment, second, gradient, step_count, old_weights, branch_rows, assignment):
    steps_f = step_count[0].astype(jnp.float32)
    first_fix = 1.0 - jnp.power(jnp.float32(0.9), steps_f)
    second_fix = 1.0 - jnp.power(jnp.float32(0.95), steps_f)
    new_moment = 0.9 * moment + 0.1 * gradient
    new_second = 0.95 * second + 0.05 * gradient * gradient
    update = new_moment / first_fix / (jnp.sqrt(new_second / second_fix) + 1e-08)
    new_master = master - learn_rate * (update + decay_rate * master)

    rows, width = new_master.shape
    chips = lax.axis_size(CHIPS)
    fresh = new_master.astype(jnp.bfloat16)
    spread = jnp.broadcast_to(fresh[None], (chips, rows, width))
    mine = lax.all_to_all(spread, CHIPS, split_axis=0, concat_axis=0, tiled=True)
    size = lax.axis_size("tp")
    me = lax.axis_index("tp")
    count = branch_rows.shape[0]
    part = old_weights.shape[1] // size
    code = lambda n: jax.ShapeDtypeStruct((n + TAIL, part), jnp.int16)
    full = jax.ShapeDtypeStruct((count, part), jnp.float32)
    ids = lax.rem(me + jnp.array([3, 5, 4], jnp.int32), size)
    q3, q5, q4a, q4b = products(
        far_kernel, branch_rows, old_weights, ids, 3, part,
        [code(count), code(count), code(count // 2), code(count // 2)],
    )
    r3, r5 = along_tp(q3, 1), along_tp(q5, -1)
    r4a, r4b = along_tp(q4a, 2), along_tp(q4b, -2)
    ids = lax.rem(me + jnp.array([1, 7, 2, 6, 0], jnp.int32), size)
    q1, q7, p2, p6, p0 = products(
        near_kernel, branch_rows, old_weights, ids, 5, part,
        [code(count), code(count), full, full, full],
    )
    r1, r7 = along_tp(q1, 1), along_tp(q7, -1)
    q2, q6 = local_call(merge_kernel, [code(count), code(count)], p2, r3, r4a, p6, r5, r4b)
    r2, r6 = along_tp(q2, 2), along_tp(q6, -2)
    replicas = lax.axis_size(PLANE)
    slots_each = 2 * count // replicas
    places = replicas * slots_each
    selector = local_call(
        selector_kernel, jax.ShapeDtypeStruct((places, count), jnp.bfloat16), assignment.reshape(1, count)
    )
    placed = local_call(
        final_kernel, jax.ShapeDtypeStruct((places, part), jnp.bfloat16), p0, r1, r7, r2, r6, selector
    )
    placed, mine = lax.optimization_barrier((placed, mine))
    placed = placed.reshape(replicas, slots_each, part)
    arrived = lax.all_to_all(placed, PLANE, split_axis=0, concat_axis=0, tiled=True)
    branch_keys = arrived.reshape(1, replicas, slots_each, part)
    other = lax.ppermute(mine, "core", [(0, 1), (1, 0)])
    core = jnp.reshape(lax.axis_index("core"), (1,)).astype(jnp.int32)
    lanes = lax.axis_size("xlo")
    mine = mine.reshape(lanes, -1, width)
    other = other.reshape(lanes, -1, width)
    pair = set_half(core, mine)
    pair = set_half(1 - core, other, pair)
    rollout_weights = pair.reshape(2 * chips * rows, width)
    return (new_master, new_moment, new_second, rollout_weights, branch_keys)


def solution(mesh):
    size = mesh.shape
    mesh = Mesh(
        mesh.devices.reshape(2, 2, 4, 2, size["tp"]), ("xlo", "core", "y", "xhi", "tp")
    )
    shard = P(("tp",) + PLANE, None)
    return jax.shard_map(
        local,
        mesh=mesh,
        in_specs=(shard, shard, shard, shard, P(), P("tp", None), P(PLANE, "tp"), P(PLANE, None)),
        out_specs=(shard, shard, shard, P("tp", None), P(PLANE, None, None, "tp")),
        check_vma=False,
    )
```

```python
import jax
import jax.numpy as jnp
from jax import lax
from jax.experimental import pallas as pl
from jax.experimental.pallas import tpu as pltpu
from jax.sharding import Mesh
from jax.sharding import PartitionSpec as P

learn_rate = 0.05
decay_rate = 0.1

PLANE = ("xlo", "core", "y", "xhi")
CHIPS = ("xlo", "y", "xhi")
LEVELS = 32767.0
TAIL = 16


def coded(value):
    top = jnp.maximum(jnp.max(jnp.abs(value), axis=0, keepdims=True), 1.2e-38)
    power = jnp.ceil(jnp.log(top) * (256.0 / 0.6931471805599453) + 0.01)
    power = jnp.clip(power, -32256.0, 32256.0)
    scaled = value * jnp.exp2(power * (-1.0 / 256.0)) * LEVELS
    codes = jnp.clip(jnp.round(scaled), -LEVELS, LEVELS)
    tail = jnp.broadcast_to(power, (TAIL, value.shape[1]))
    return codes.astype(jnp.int32).astype(jnp.int16), tail.astype(jnp.int32).astype(jnp.int16)


def put_coded(ref, value):
    codes, tail = coded(value)
    rows = value.shape[0]
    ref[0:rows, :] = codes
    ref[rows : rows + TAIL, :] = tail


def take_coded(ref):
    rows = ref.shape[0] - TAIL
    power = ref[rows : rows + TAIL, :].astype(jnp.int32).astype(jnp.float32)[0:1, :]
    codes = ref[0:rows, :].astype(jnp.int32).astype(jnp.float32)
    return codes * (1.0 / LEVELS) * jnp.exp2(power * (1.0 / 256.0))


def products_kernel(ids, x_hbm, w_hbm, up, down, far_up, far_down, next_up, next_down, own, x, w, x_sem, w_sems):
    depth, part = w.shape[1], w.shape[2] // 2
    half = x.shape[0] // 2
    load = pltpu.make_async_copy(x_hbm, x, x_sem)
    load.start()
    loads = []
    for k in range(8):
        column = pl.multiple_of(ids[k] * part, part)
        loads.append(
            pltpu.make_async_copy(
                w_hbm.at[:, pl.ds(column, part)],
                w.at[k // 2, :, pl.ds(k % 2 * part, part)],
                w_sems.at[k],
            )
        )
        loads[-1].start()
    load.wait()

    def pair(k):
        loads[2 * k].wait()
        loads[2 * k + 1].wait()
        both = jnp.dot(x[...], w[k], preferred_element_type=jnp.float32)
        return both[:, :part], both[:, part:]

    for k, out in enumerate((up, down)):
        for i, value in enumerate(pair(k)):
            put_coded(out.at[i], value)
    far, mine = pair(2)
    put_coded(far_up, far[:half])
    put_coded(far_down, far[half:])
    own[...] = mine
    next_up[...], next_down[...] = pair(3)


def products(x, w, ids, outs):
    rows, depth = x.shape
    width = w.shape[1] // 4
    return pl.pallas_call(
        products_kernel,
        out_shape=outs,
        in_specs=[pl.BlockSpec(memory_space=pltpu.SMEM)] + [pl.BlockSpec(memory_space=pl.ANY)] * 2,
        out_specs=[pl.BlockSpec(memory_space=pltpu.VMEM)] * len(outs),
        scratch_shapes=[
            pltpu.VMEM((rows, depth), x.dtype),
            pltpu.VMEM((4, depth, width), w.dtype),
            pltpu.SemaphoreType.DMA,
            pltpu.SemaphoreType.DMA((8,)),
        ],
        compiler_params=pltpu.CompilerParams(vmem_limit_bytes=60 * 2**20),
        cost_estimate=pl.CostEstimate(
            flops=2 * rows * depth * w.shape[1], bytes_accessed=2 * (x.size + w.size), transcendentals=0
        ),
    )(ids, x, w)


def update_kernel(step_ref, master, moment, second, gradient, new_master, new_moment, new_second, spread):
    def times(k, fixes):
        return fixes[0] * 0.9, fixes[1] * 0.95

    one = jnp.float32(1.0)
    first, other = lax.fori_loop(0, step_ref[0], times, (one, one))
    first_fix, second_fix = 1.0 - first, 1.0 - other
    g, old = gradient[...], master[...]
    m = 0.9 * moment[...] + 0.1 * g
    v = 0.95 * second[...] + 0.05 * g * g
    ones = jnp.ones((1, g.shape[1]), jnp.float32)
    update = m / (ones * first_fix) / (jnp.sqrt(v / (ones * second_fix)) + 1e-08)
    new = old - learn_rate * (update + decay_rate * old)
    new_moment[...] = m
    new_second[...] = v
    new_master[...] = new
    fresh = new.astype(jnp.bfloat16)
    for k in range(spread.shape[0]):
        spread[k] = fresh


def updated(step_count, master, moment, second, gradient, chips):
    same = jax.ShapeDtypeStruct(master.shape, jnp.float32)
    return pl.pallas_call(
        update_kernel,
        out_shape=[same, same, same, jax.ShapeDtypeStruct((chips,) + master.shape, jnp.bfloat16)],
        in_specs=[pl.BlockSpec(memory_space=pltpu.SMEM)] + [pl.BlockSpec(master.shape, lambda: (0, 0))] * 4,
        out_specs=[pl.BlockSpec(master.shape, lambda: (0, 0))] * 3 + [pl.BlockSpec((chips,) + master.shape, lambda: (0, 0, 0))],
        compiler_params=pltpu.CompilerParams(vmem_limit_bytes=60 * 2**20),
        cost_estimate=pl.CostEstimate(
            flops=30 * master.size, bytes_accessed=28 * master.size, transcendentals=3 * master.size
        ),
    )(step_count, master, moment, second, gradient)


def local_call(kernel, outs, *args, flops=0):
    return pl.pallas_call(
        kernel,
        out_shape=outs,
        compiler_params=pltpu.CompilerParams(vmem_limit_bytes=40 * 2**20),
        cost_estimate=pl.CostEstimate(flops=flops, bytes_accessed=2**20, transcendentals=0),
    )(*args)


def merge_kernel(own_a, next_a, far_a, own_b, next_b, far_b, qa, qb):
    half = own_a.shape[0] // 2
    total = own_a[...] + take_coded(next_a.at[0])
    total = jnp.concatenate([total[:half] + take_coded(far_a), total[half:]], axis=0)
    put_coded(qa, total)
    total = own_b[...] + take_coded(next_b.at[0])
    total = jnp.concatenate([total[:half], total[half:] + take_coded(far_b)], axis=0)
    put_coded(qb, total)


def selector_kernel(target_ref, out):
    places, rows = out.shape
    replicas = 32
    each = places // replicas
    target = target_ref[...]
    onehot = (lax.broadcasted_iota(jnp.int32, (replicas, rows), 0) == target).astype(jnp.float32)
    before = (
        lax.broadcasted_iota(jnp.int32, (rows, rows), 0)
        < lax.broadcasted_iota(jnp.int32, (rows, rows), 1)
    ).astype(jnp.bfloat16)
    ranks = jnp.dot(onehot.astype(jnp.bfloat16), before, preferred_element_type=jnp.float32)
    rank = jnp.sum(ranks * onehot, axis=0, keepdims=True).astype(jnp.int32)
    position = target * each + rank
    out[...] = (lax.broadcasted_iota(jnp.int32, (places, rows), 0) == position).astype(jnp.float32).astype(jnp.bfloat16)


def final_kernel(own, ra, rb, rc, rd, selector, out):
    keys = own[...] + take_coded(ra.at[1]) + take_coded(rb.at[1]) + take_coded(rc) + take_coded(rd)
    out[...] = jnp.dot(
        selector[...], keys.astype(jnp.bfloat16), preferred_element_type=jnp.float32
    ).astype(jnp.bfloat16)


def half_kernel(place, half, *refs):
    refs[-1][...] = half[...].reshape(refs[-1].shape)


def set_half(place, half, pair=None):
    lanes, rows, width = half.shape
    step = rows // 2
    args = (place, half) + (() if pair is None else (pair,))
    return pl.pallas_call(
        half_kernel,
        out_shape=jax.ShapeDtypeStruct((lanes, 2, rows, width), half.dtype),
        grid_spec=pltpu.PrefetchScalarGridSpec(
            num_scalar_prefetch=1,
            grid=(lanes, rows // step),
            in_specs=[pl.BlockSpec((1, step, width), lambda i, j, place: (i, j, 0))]
            + [pl.BlockSpec(memory_space=pl.ANY)] * (len(args) - 2),
            out_specs=pl.BlockSpec((1, 1, step, width), lambda i, j, place: (i, place[0], j, 0)),
        ),
        input_output_aliases={} if pair is None else {2: 0},
        compiler_params=pltpu.CompilerParams(vmem_limit_bytes=16 * 2**20),
        cost_estimate=pl.CostEstimate(flops=0, bytes_accessed=4 * half.size, transcendentals=0),
    )(*args)


def along_tp(value, step):
    size = lax.axis_size("tp")
    return lax.ppermute(value, "tp", [(i, (i + step) % size) for i in range(size)])


def local(master, moment, second, gradient, step_count, old_weights, branch_rows, assignment):
    rows, width = master.shape
    chips = lax.axis_size(CHIPS)
    new_master, new_moment, new_second, spread = updated(
        step_count, master, moment, second, gradient, chips
    )
    mine = lax.all_to_all(spread, CHIPS, split_axis=0, concat_axis=0, tiled=True)

    size = lax.axis_size("tp")
    me = lax.axis_index("tp")
    count = branch_rows.shape[0]
    part = old_weights.shape[1] // size
    code = lambda *n: jax.ShapeDtypeStruct(n[:-1] + (n[-1] + TAIL, part), jnp.int16)
    full = jax.ShapeDtypeStruct((count, part), jnp.float32)
    ids = lax.rem(me + jnp.array([3, 1, 5, 7, 4, 0, 2, 6], jnp.int32), size)
    up, down, far_up, far_down, p2, p6, p0 = products(
        branch_rows, old_weights, ids,
        [code(2, count), code(2, count), code(count // 2), code(count // 2), full, full, full],
    )
    up, down = along_tp(up, 1), along_tp(down, -1)
    far_up, far_down = along_tp(far_up, 2), along_tp(far_down, -2)
    q2, q6 = local_call(
        merge_kernel, [code(count), code(count)], p2, up, far_up, p6, down, far_down
    )
    r2, r6 = along_tp(q2, 2), along_tp(q6, -2)
    r2, mine = lax.optimization_barrier((r2, mine))
    replicas = lax.axis_size(PLANE)
    slots_each = 2 * count // replicas
    places = replicas * slots_each
    selector = local_call(
        selector_kernel, jax.ShapeDtypeStruct((places, count), jnp.bfloat16), assignment.reshape(1, count)
    )
    placed = local_call(
        final_kernel, jax.ShapeDtypeStruct((places, part), jnp.bfloat16), p0, up, down, r2, r6, selector
    )
    placed = placed.reshape(replicas, slots_each, part)
    arrived = lax.all_to_all(placed, PLANE, split_axis=0, concat_axis=0, tiled=True)
    branch_keys = arrived.reshape(1, replicas, slots_each, part)
    other = lax.ppermute(mine, "core", [(0, 1), (1, 0)])
    core = jnp.reshape(lax.axis_index("core"), (1,)).astype(jnp.int32)
    lanes = lax.axis_size("xlo")
    mine = mine.reshape(lanes, -1, width)
    other = other.reshape(lanes, -1, width)
    pair = set_half(core, mine)
    pair = set_half(1 - core, other, pair)
    rollout_weights = pair.reshape(2 * chips * rows, width)
    return (new_master, new_moment, new_second, rollout_weights, branch_keys)


def solution(mesh):
    size = mesh.shape
    mesh = Mesh(
        mesh.devices.reshape(2, 2, 4, 2, size["tp"]), ("xlo", "core", "y", "xhi", "tp")
    )
    shard = P(("tp",) + PLANE, None)
    return jax.shard_map(
        local,
        mesh=mesh,
        in_specs=(shard, shard, shard, shard, P(), P("tp", None), P(PLANE, "tp"), P(PLANE, None)),
        out_specs=(shard, shard, shard, P("tp", None), P(PLANE, None, None, "tp")),
        check_vma=False,
    )
```

```python
import functools

import jax
import jax.numpy as jnp
from jax import lax
from jax.experimental import pallas as pl
from jax.experimental.pallas import tpu as pltpu
from jax.sharding import Mesh
from jax.sharding import PartitionSpec as P

learn_rate = 0.05
decay_rate = 0.1

PLANE = ("xlo", "core", "y", "xhi")
CHIPS = ("xlo", "y", "xhi")
LEVELS = 32767.0
TAIL = 16


def coded(value):
    top = jnp.maximum(jnp.max(jnp.abs(value), axis=0, keepdims=True), 1.2e-38)
    power = jnp.ceil(jnp.log(top) * (256.0 / 0.6931471805599453) + 0.01)
    power = jnp.clip(power, -32256.0, 32256.0)
    scaled = value * jnp.exp2(power * (-1.0 / 256.0)) * LEVELS
    codes = jnp.clip(jnp.round(scaled), -LEVELS, LEVELS)
    tail = jnp.broadcast_to(power, (TAIL, value.shape[1]))
    return codes.astype(jnp.int32).astype(jnp.int16), tail.astype(jnp.int32).astype(jnp.int16)


def put_coded(ref, value):
    codes, tail = coded(value)
    rows = value.shape[0]
    ref[0:rows, :] = codes
    ref[rows : rows + TAIL, :] = tail


def take_coded(ref):
    rows = ref.shape[0] - TAIL
    power = ref[rows : rows + TAIL, :].astype(jnp.int32).astype(jnp.float32)[0:1, :]
    codes = ref[0:rows, :].astype(jnp.int32).astype(jnp.float32)
    return codes * (1.0 / LEVELS) * jnp.exp2(power * (1.0 / 256.0))


def product(rows_ref, columns_ref):
    return jnp.dot(rows_ref[...], columns_ref[...], preferred_element_type=jnp.float32)


def pair_product(rows_ref, first_ref, second_ref):
    part = first_ref.shape[1]
    columns = jnp.concatenate([first_ref[...], second_ref[...]], axis=1)
    both = jnp.dot(rows_ref[...], columns, preferred_element_type=jnp.float32)
    return both[:, :part], both[:, part:]


def head_kernel(
    step_ref, ids, master_h, moment_h, second_h, gradient_h, x_h, w_h,
    new_master_h, new_moment_h, new_second_h, spread_h, up_h, down_h, far_up_h, far_down_h,
    master, moment, second, gradient, new_master, new_moment, new_second, fresh,
    x, wa, wb, wc, up, down, far_up, far_down, sems, out_sems, spread_sems,
):
    part = wa.shape[1]
    half = x.shape[0] // 2
    columns = [w_h.at[:, pl.ds(pl.multiple_of(ids[k] * part, part), part)] for k in range(3)]
    sources = [master_h, moment_h, second_h, gradient_h, x_h] + columns
    places = [master, moment, second, gradient, x, wa, wb, wc]
    loads = [
        pltpu.make_async_copy(source, place, sems.at[k])
        for k, (source, place) in enumerate(zip(sources, places))
    ]
    for load in loads:
        load.start()

    def times(k, fixes):
        return fixes[0] * 0.9, fixes[1] * 0.95

    one = jnp.float32(1.0)
    first, other = lax.fori_loop(0, step_ref[0], times, (one, one))
    for load in loads[:4]:
        load.wait()
    ones = jnp.ones((1, master.shape[1]), jnp.float32)
    first_fix, second_fix = ones * (1.0 - first), ones * (1.0 - other)
    g, old = gradient[...], master[...]
    m = 0.9 * moment[...] + 0.1 * g
    v = 0.95 * second[...] + 0.05 * g * g
    update = m / first_fix / (jnp.sqrt(v / second_fix) + 1e-08)
    new = old - learn_rate * (update + decay_rate * old)
    new_moment[...] = m
    new_second[...] = v
    new_master[...] = new
    fresh[...] = new.astype(jnp.bfloat16)
    stores = [
        pltpu.make_async_copy(fresh, spread_h.at[k], spread_sems.at[k])
        for k in range(spread_h.shape[0])
    ]
    finished = [(new_master, new_master_h), (new_moment, new_moment_h), (new_second, new_second_h)]
    stores += [
        pltpu.make_async_copy(source, place, out_sems.at[k])
        for k, (source, place) in enumerate(finished)
    ]
    for store in stores:
        store.start()

    def send(k, source, place):
        store = pltpu.make_async_copy(source, place, out_sems.at[3 + k])
        store.start()
        stores.append(store)

    for load in loads[4:7]:
        load.wait()
    above, below = pair_product(x, wa, wb)
    put_coded(up, above)
    send(0, up, up_h)
    put_coded(down, below)
    send(1, down, down_h)
    loads[7].wait()
    far = product(x, wc)
    put_coded(far_up, far[:half])
    send(2, far_up, far_up_h)
    put_coded(far_down, far[half:])
    send(3, far_down, far_down_h)
    for store in stores:
        store.wait()


def head(step_count, ids, master, moment, second, gradient, x, w, chips):
    rows, depth = x.shape
    part = w.shape[1] // 8
    anywhere = pl.BlockSpec(memory_space=pl.ANY)
    scalar = pl.BlockSpec(memory_space=pltpu.SMEM)
    shard = master.shape
    codes = [(rows + TAIL, part)] * 2 + [(rows // 2 + TAIL, part)] * 2
    outs = [jax.ShapeDtypeStruct(shard, jnp.float32)] * 3
    outs += [jax.ShapeDtypeStruct((chips,) + shard, jnp.bfloat16)]
    outs += [jax.ShapeDtypeStruct(c, jnp.int16) for c in codes]
    return pl.pallas_call(
        head_kernel,
        out_shape=outs,
        in_specs=[scalar] * 2 + [anywhere] * 6,
        out_specs=[anywhere] * len(outs),
        scratch_shapes=[pltpu.VMEM(shard, jnp.float32)] * 7
        + [pltpu.VMEM(shard, jnp.bfloat16), pltpu.VMEM((rows, depth), x.dtype)]
        + [pltpu.VMEM((depth, part), w.dtype)] * 3
        + [pltpu.VMEM(c, jnp.int16) for c in codes]
        + [
            pltpu.SemaphoreType.DMA((8,)),
            pltpu.SemaphoreType.DMA((7,)),
            pltpu.SemaphoreType.DMA((chips,)),
        ],
        compiler_params=pltpu.CompilerParams(vmem_limit_bytes=60 * 2**20),
        cost_estimate=pl.CostEstimate(
            flops=6 * rows * depth * part + 30 * master.size,
            bytes_accessed=2 * x.size + 6 * depth * part + 60 * master.size,
            transcendentals=3 * master.size,
        ),
    )(step_count, ids, master, moment, second, gradient, x, w)


def near_kernel(ids, x, wa, wb, wc, wd, we, qa, qb, pc, pd, pe):
    above, below = pair_product(x, wa, wb)
    put_coded(qa, above)
    put_coded(qb, below)
    pc[...], pd[...] = pair_product(x, wc, wd)
    pe[...] = product(x, we)


def products(kernel, x, w, ids, count, width, outs):
    rows, depth = x.shape
    whole = lambda g, ids: (0, 0)
    columns = [
        pl.BlockSpec((depth, width), functools.partial(lambda k, g, ids: (0, ids[k]), k))
        for k in range(count)
    ]
    return pl.pallas_call(
        kernel,
        out_shape=outs,
        grid_spec=pltpu.PrefetchScalarGridSpec(
            num_scalar_prefetch=1,
            grid=(1,),
            in_specs=[pl.BlockSpec((rows, depth), whole)] + columns,
            out_specs=[pl.BlockSpec(o.shape, whole) for o in outs],
        ),
        compiler_params=pltpu.CompilerParams(vmem_limit_bytes=40 * 2**20),
        cost_estimate=pl.CostEstimate(
            flops=2 * rows * depth * width * count,
            bytes_accessed=2 * depth * (rows + width * count),
            transcendentals=0,
        ),
    )(ids, x, *([w] * count))


def local_call(kernel, outs, *args, flops=0):
    return pl.pallas_call(
        kernel,
        out_shape=outs,
        compiler_params=pltpu.CompilerParams(vmem_limit_bytes=40 * 2**20),
        cost_estimate=pl.CostEstimate(flops=flops, bytes_accessed=2**20, transcendentals=0),
    )(*args)


def merge_kernel(own_a, next_a, far_a, own_b, next_b, far_b, qa, qb):
    half = own_a.shape[0] // 2
    total = own_a[...] + take_coded(next_a)
    total = jnp.concatenate([total[:half] + take_coded(far_a), total[half:]], axis=0)
    put_coded(qa, total)
    total = own_b[...] + take_coded(next_b)
    total = jnp.concatenate([total[:half], total[half:] + take_coded(far_b)], axis=0)
    put_coded(qb, total)


def selector_kernel(target_ref, out):
    places, rows = out.shape
    replicas = 32
    each = places // replicas
    target = target_ref[...]
    onehot = (lax.broadcasted_iota(jnp.int32, (replicas, rows), 0) == target).astype(jnp.float32)
    before = (
        lax.broadcasted_iota(jnp.int32, (rows, rows), 0)
        < lax.broadcasted_iota(jnp.int32, (rows, rows), 1)
    ).astype(jnp.bfloat16)
    ranks = jnp.dot(onehot.astype(jnp.bfloat16), before, preferred_element_type=jnp.float32)
    rank = jnp.sum(ranks * onehot, axis=0, keepdims=True).astype(jnp.int32)
    position = target * each + rank
    out[...] = (lax.broadcasted_iota(jnp.int32, (places, rows), 0) == position).astype(jnp.float32).astype(jnp.bfloat16)


def final_kernel(own, ra, rb, rc, rd, selector, out):
    keys = own[...] + take_coded(ra) + take_coded(rb) + take_coded(rc) + take_coded(rd)
    out[...] = jnp.dot(
        selector[...], keys.astype(jnp.bfloat16), preferred_element_type=jnp.float32
    ).astype(jnp.bfloat16)


def half_kernel(place, half, *refs):
    refs[-1][...] = half[...].reshape(refs[-1].shape)


def set_half(place, half, pair=None):
    lanes, rows, width = half.shape
    step = rows // 2
    args = (place, half) + (() if pair is None else (pair,))
    return pl.pallas_call(
        half_kernel,
        out_shape=jax.ShapeDtypeStruct((lanes, 2, rows, width), half.dtype),
        grid_spec=pltpu.PrefetchScalarGridSpec(
            num_scalar_prefetch=1,
            grid=(lanes, rows // step),
            in_specs=[pl.BlockSpec((1, step, width), lambda i, j, place: (i, j, 0))]
            + [pl.BlockSpec(memory_space=pl.ANY)] * (len(args) - 2),
            out_specs=pl.BlockSpec((1, 1, step, width), lambda i, j, place: (i, place[0], j, 0)),
        ),
        input_output_aliases={} if pair is None else {2: 0},
        compiler_params=pltpu.CompilerParams(vmem_limit_bytes=16 * 2**20),
        cost_estimate=pl.CostEstimate(flops=0, bytes_accessed=4 * half.size, transcendentals=0),
    )(*args)


def along_tp(value, step):
    size = lax.axis_size("tp")
    return lax.ppermute(value, "tp", [(i, (i + step) % size) for i in range(size)])


def local(master, moment, second, gradient, step_count, old_weights, branch_rows, assignment):
    rows, width = master.shape
    chips = lax.axis_size(CHIPS)
    size = lax.axis_size("tp")
    me = lax.axis_index("tp")
    count = branch_rows.shape[0]
    part = old_weights.shape[1] // size
    code = lambda n: jax.ShapeDtypeStruct((n + TAIL, part), jnp.int16)
    full = jax.ShapeDtypeStruct((count, part), jnp.float32)
    at = lambda *steps: jnp.stack([lax.rem(me + k, size) for k in steps]).astype(jnp.int32)
    new_master, new_moment, new_second, spread, q3, q5, q4a, q4b = head(
        step_count, at(3, 5, 4), master, moment, second, gradient, branch_rows, old_weights, chips
    )
    mine = lax.all_to_all(spread, CHIPS, split_axis=0, concat_axis=0, tiled=True)
    r3, r5 = along_tp(q3, 1), along_tp(q5, -1)
    r4a, r4b = along_tp(q4a, 2), along_tp(q4b, -2)
    q1, q7, p2, p6, p0 = products(
        near_kernel, branch_rows, old_weights, at(1, 7, 2, 6, 0), 5, part,
        [code(count), code(count), full, full, full],
    )
    r1, r7 = along_tp(q1, 1), along_tp(q7, -1)
    q2, q6 = local_call(merge_kernel, [code(count), code(count)], p2, r3, r4a, p6, r5, r4b)
    r2, r6 = along_tp(q2, 2), along_tp(q6, -2)
    replicas = lax.axis_size(PLANE)
    slots_each = 2 * count // replicas
    places = replicas * slots_each
    selector = local_call(
        selector_kernel, jax.ShapeDtypeStruct((places, count), jnp.bfloat16), assignment.reshape(1, count)
    )
    placed = local_call(
        final_kernel, jax.ShapeDtypeStruct((places, part), jnp.bfloat16), p0, r1, r7, r2, r6, selector
    )
    mine, _ = lax.optimization_barrier((mine, placed))
    placed = placed.reshape(replicas, slots_each, part)
    arrived = lax.all_to_all(placed, PLANE, split_axis=0, concat_axis=0, tiled=True)
    other = lax.ppermute(mine, "core", [(0, 1), (1, 0)])
    core = jnp.reshape(lax.axis_index("core"), (1,)).astype(jnp.int32)
    lanes = lax.axis_size("xlo")
    mine = mine.reshape(lanes, -1, width)
    other = other.reshape(lanes, -1, width)
    pair = set_half(core, mine)
    pair = set_half(1 - core, other, pair)
    pair, arrived = lax.optimization_barrier((pair, arrived))
    branch_keys = arrived.reshape(1, replicas, slots_each, part)
    rollout_weights = pair.reshape(2 * chips * rows, width)
    return (new_master, new_moment, new_second, rollout_weights, branch_keys)


def solution(mesh):
    size = mesh.shape
    mesh = Mesh(
        mesh.devices.reshape(2, 2, 4, 2, size["tp"]), ("xlo", "core", "y", "xhi", "tp")
    )
    shard = P(("tp",) + PLANE, None)
    return jax.shard_map(
        local,
        mesh=mesh,
        in_specs=(shard, shard, shard, shard, P(), P("tp", None), P(PLANE, "tp"), P(PLANE, None)),
        out_specs=(shard, shard, shard, P("tp", None), P(PLANE, None, None, "tp")),
        check_vma=False,
    )
```

```python
import functools

import jax
import jax.numpy as jnp
from jax import lax
from jax.experimental import pallas as pl
from jax.experimental.pallas import tpu as pltpu
from jax.sharding import Mesh
from jax.sharding import PartitionSpec as P

learn_rate = 0.05
decay_rate = 0.1

PLANE = ("xlo", "core", "y", "xhi")
CHIPS = ("xlo", "y", "xhi")
LEVELS = 32767.0
TAIL = 16


def coded(value):
    top = jnp.maximum(jnp.max(jnp.abs(value), axis=0, keepdims=True), 1.2e-38)
    power = jnp.ceil(jnp.log(top) * (256.0 / 0.6931471805599453) + 0.01)
    power = jnp.clip(power, -32256.0, 32256.0)
    scaled = value * jnp.exp2(power * (-1.0 / 256.0)) * LEVELS
    codes = jnp.clip(jnp.round(scaled), -LEVELS, LEVELS)
    tail = jnp.broadcast_to(power, (TAIL, value.shape[1]))
    return codes.astype(jnp.int32).astype(jnp.int16), tail.astype(jnp.int32).astype(jnp.int16)


def put_coded(ref, value):
    codes, tail = coded(value)
    rows = value.shape[0]
    ref[0:rows, :] = codes
    ref[rows : rows + TAIL, :] = tail


def take_coded(ref):
    rows = ref.shape[0] - TAIL
    power = ref[rows : rows + TAIL, :].astype(jnp.int32).astype(jnp.float32)[0:1, :]
    codes = ref[0:rows, :].astype(jnp.int32).astype(jnp.float32)
    return codes * (1.0 / LEVELS) * jnp.exp2(power * (1.0 / 256.0))


def product(rows_ref, columns_ref):
    return jnp.dot(rows_ref[...], columns_ref[...], preferred_element_type=jnp.float32)


def pair_product(rows_ref, first_ref, second_ref):
    part = first_ref.shape[1]
    columns = jnp.concatenate([first_ref[...], second_ref[...]], axis=1)
    both = jnp.dot(rows_ref[...], columns, preferred_element_type=jnp.float32)
    return both[:, :part], both[:, part:]


def update_kernel(
    step_ref, master_h, moment_h, second_h, gradient_h,
    new_master_h, new_moment_h, new_second_h, spread_h,
    master, moment, second, gradient, new_master, new_moment, new_second, fresh, sems, out_sems, spread_sems,
):
    sources = [moment_h, gradient_h, second_h, master_h]
    places = [moment, gradient, second, master]
    loads = [
        pltpu.make_async_copy(source, place, sems.at[k])
        for k, (source, place) in enumerate(zip(sources, places))
    ]
    for load in loads:
        load.start()

    def times(k, fixes):
        return fixes[0] * 0.9, fixes[1] * 0.95

    one = jnp.float32(1.0)
    first, other = lax.fori_loop(0, step_ref[0], times, (one, one))
    ones = jnp.ones((1, master.shape[1]), jnp.float32)
    first_fix, second_fix = ones * (1.0 - first), ones * (1.0 - other)
    for load in loads:
        load.wait()
    g, old = gradient[...], master[...]
    m = 0.9 * moment[...] + 0.1 * g
    v = 0.95 * second[...] + 0.05 * g * g
    update = m / first_fix / (jnp.sqrt(v / second_fix) + 1e-08)
    new = old - learn_rate * (update + decay_rate * old)
    fresh[...] = new.astype(jnp.bfloat16)
    new_moment[...] = m
    new_second[...] = v
    new_master[...] = new
    stores = [
        pltpu.make_async_copy(fresh, spread_h.at[k], spread_sems.at[k])
        for k in range(spread_h.shape[0])
    ]
    finished = [(new_master, new_master_h), (new_moment, new_moment_h), (new_second, new_second_h)]
    stores += [
        pltpu.make_async_copy(source, place, out_sems.at[k])
        for k, (source, place) in enumerate(finished)
    ]
    for store in stores:
        store.start()
    for store in stores:
        store.wait()


def updated(step_count, master, moment, second, gradient, chips):
    anywhere = pl.BlockSpec(memory_space=pl.ANY)
    shard = master.shape
    outs = [jax.ShapeDtypeStruct(shard, jnp.float32)] * 3
    outs += [jax.ShapeDtypeStruct((chips,) + shard, jnp.bfloat16)]
    return pl.pallas_call(
        update_kernel,
        out_shape=outs,
        in_specs=[pl.BlockSpec(memory_space=pltpu.SMEM)] + [anywhere] * 4,
        out_specs=[anywhere] * 4,
        scratch_shapes=[pltpu.VMEM(shard, jnp.float32)] * 7
        + [
            pltpu.VMEM(shard, jnp.bfloat16),
            pltpu.SemaphoreType.DMA((4,)),
            pltpu.SemaphoreType.DMA((3,)),
            pltpu.SemaphoreType.DMA((chips,)),
        ],
        compiler_params=pltpu.CompilerParams(vmem_limit_bytes=60 * 2**20),
        cost_estimate=pl.CostEstimate(
            flops=30 * master.size, bytes_accessed=60 * master.size, transcendentals=3 * master.size
        ),
    )(step_count, master, moment, second, gradient)


def loading(steps, kernel, me, x_h, w_h, *refs):
    x, w, x_sems, w_sems = refs[-4:]
    part = w.shape[2]
    rows = x.shape[0] // 2
    loads = []
    for k in range(2):
        half = pl.ds(k * rows, rows)
        loads.append(pltpu.make_async_copy(x_h.at[half], x.at[half], x_sems.at[k]))
    for k, step in enumerate(steps):
        block = lax.rem(me[0] + step, w_h.shape[1] // part)
        columns = pl.ds(pl.multiple_of(block * part, part), part)
        loads.append(pltpu.make_async_copy(w_h.at[:, columns], w.at[k], w_sems.at[k]))
    for load in loads:
        load.start()
    for load in loads[:2]:
        load.wait()

    def columns(k):
        loads[2 + k].wait()
        return w.at[k]

    kernel(x, columns, *refs[:-4])


def far_kernel(x, columns, up, down, far_up, far_down):
    half = x.shape[0] // 2
    above, below = pair_product(x, columns(0), columns(1))
    put_coded(up, above)
    put_coded(down, below)
    far = product(x, columns(2))
    put_coded(far_up, far[:half])
    put_coded(far_down, far[half:])


def near_kernel(x, columns, up, down, next_up, next_down, own):
    above, below = pair_product(x, columns(0), columns(1))
    put_coded(up, above)
    put_coded(down, below)
    next_up[...], next_down[...] = pair_product(x, columns(2), columns(3))
    own[...] = product(x, columns(4))


def products(kernel, x, w, me, steps, outs):
    rows, depth = x.shape
    count = len(steps)
    part = w.shape[1] // 8
    anywhere = pl.BlockSpec(memory_space=pl.ANY)
    return pl.pallas_call(
        functools.partial(loading, steps, kernel),
        out_shape=outs,
        in_specs=[pl.BlockSpec(memory_space=pltpu.SMEM), anywhere, anywhere],
        out_specs=[pl.BlockSpec(memory_space=pltpu.VMEM)] * len(outs),
        scratch_shapes=[
            pltpu.VMEM((rows, depth), x.dtype),
            pltpu.VMEM((count, depth, part), w.dtype),
            pltpu.SemaphoreType.DMA((2,)),
            pltpu.SemaphoreType.DMA((count,)),
        ],
        compiler_params=pltpu.CompilerParams(vmem_limit_bytes=52 * 2**20),
        cost_estimate=pl.CostEstimate(
            flops=2 * rows * depth * part * count,
            bytes_accessed=2 * depth * (rows + part * count),
            transcendentals=0,
        ),
    )(me, x, w)


def local_call(kernel, outs, *args, flops=0):
    return pl.pallas_call(
        kernel,
        out_shape=outs,
        compiler_params=pltpu.CompilerParams(vmem_limit_bytes=40 * 2**20),
        cost_estimate=pl.CostEstimate(flops=flops, bytes_accessed=2**20, transcendentals=0),
    )(*args)


def merge_kernel(own_a, next_a, far_a, own_b, next_b, far_b, qa, qb):
    half = own_a.shape[0] // 2
    total = own_a[...] + take_coded(next_a)
    total = jnp.concatenate([total[:half] + take_coded(far_a), total[half:]], axis=0)
    put_coded(qa, total)
    total = own_b[...] + take_coded(next_b)
    total = jnp.concatenate([total[:half], total[half:] + take_coded(far_b)], axis=0)
    put_coded(qb, total)


def selector_kernel(target_ref, out):
    places, rows = out.shape
    replicas = 32
    each = places // replicas
    target = target_ref[...]
    onehot = (lax.broadcasted_iota(jnp.int32, (replicas, rows), 0) == target).astype(jnp.float32)
    before = (
        lax.broadcasted_iota(jnp.int32, (rows, rows), 0)
        < lax.broadcasted_iota(jnp.int32, (rows, rows), 1)
    ).astype(jnp.bfloat16)
    ranks = jnp.dot(onehot.astype(jnp.bfloat16), before, preferred_element_type=jnp.float32)
    rank = jnp.sum(ranks * onehot, axis=0, keepdims=True).astype(jnp.int32)
    position = target * each + rank
    out[...] = (lax.broadcasted_iota(jnp.int32, (places, rows), 0) == position).astype(jnp.float32).astype(jnp.bfloat16)


def final_kernel(own, ra, rb, rc, rd, selector, out):
    keys = own[...] + take_coded(ra) + take_coded(rb) + take_coded(rc) + take_coded(rd)
    out[...] = jnp.dot(
        selector[...], keys.astype(jnp.bfloat16), preferred_element_type=jnp.float32
    ).astype(jnp.bfloat16)


def half_kernel(place, half, *refs):
    refs[-1][...] = half[...].reshape(refs[-1].shape)


def set_half(place, half, pair=None):
    lanes, rows, width = half.shape
    step = rows // 2
    args = (place, half) + (() if pair is None else (pair,))
    return pl.pallas_call(
        half_kernel,
        out_shape=jax.ShapeDtypeStruct((lanes, 2, rows, width), half.dtype),
        grid_spec=pltpu.PrefetchScalarGridSpec(
            num_scalar_prefetch=1,
            grid=(lanes, rows // step),
            in_specs=[pl.BlockSpec((1, step, width), lambda i, j, place: (i, j, 0))]
            + [pl.BlockSpec(memory_space=pl.ANY)] * (len(args) - 2),
            out_specs=pl.BlockSpec((1, 1, step, width), lambda i, j, place: (i, place[0], j, 0)),
        ),
        input_output_aliases={} if pair is None else {2: 0},
        compiler_params=pltpu.CompilerParams(vmem_limit_bytes=16 * 2**20),
        cost_estimate=pl.CostEstimate(flops=0, bytes_accessed=4 * half.size, transcendentals=0),
    )(*args)


def along_tp(value, step):
    size = lax.axis_size("tp")
    return lax.ppermute(value, "tp", [(i, (i + step) % size) for i in range(size)])


def local(master, moment, second, gradient, step_count, old_weights, branch_rows, assignment):
    rows, width = master.shape
    chips = lax.axis_size(CHIPS)
    size = lax.axis_size("tp")
    me = jnp.reshape(lax.axis_index("tp"), (1,)).astype(jnp.int32)
    count = branch_rows.shape[0]
    part = old_weights.shape[1] // size
    code = lambda n: jax.ShapeDtypeStruct((n + TAIL, part), jnp.int16)
    full = jax.ShapeDtypeStruct((count, part), jnp.float32)
    new_master, new_moment, new_second, spread = updated(
        step_count, master, moment, second, gradient, chips
    )
    mine = lax.all_to_all(spread, CHIPS, split_axis=0, concat_axis=0, tiled=True)
    q3, q5, q4a, q4b = products(
        far_kernel, branch_rows, old_weights, me, (3, 5, 4),
        [code(count), code(count), code(count // 2), code(count // 2)],
    )
    r3, r5 = along_tp(q3, 1), along_tp(q5, -1)
    r4a, r4b = along_tp(q4a, 2), along_tp(q4b, -2)
    q1, q7, p2, p6, p0 = products(
        near_kernel, branch_rows, old_weights, me, (1, 7, 2, 6, 0),
        [code(count), code(count), full, full, full],
    )
    r1, r7 = along_tp(q1, 1), along_tp(q7, -1)
    q2, q6 = local_call(merge_kernel, [code(count), code(count)], p2, r3, r4a, p6, r5, r4b)
    r2, r6 = along_tp(q2, 2), along_tp(q6, -2)
    replicas = lax.axis_size(PLANE)
    slots_each = 2 * count // replicas
    places = replicas * slots_each
    selector = local_call(
        selector_kernel, jax.ShapeDtypeStruct((places, count), jnp.bfloat16), assignment.reshape(1, count)
    )
    placed = local_call(
        final_kernel, jax.ShapeDtypeStruct((places, part), jnp.bfloat16), p0, r1, r7, r2, r6, selector
    )
    mine, _ = lax.optimization_barrier((mine, placed))
    placed = placed.reshape(replicas, slots_each, part)
    arrived = lax.all_to_all(placed, PLANE, split_axis=0, concat_axis=0, tiled=True)
    other = lax.ppermute(mine, "core", [(0, 1), (1, 0)])
    core = jnp.reshape(lax.axis_index("core"), (1,)).astype(jnp.int32)
    lanes = lax.axis_size("xlo")
    mine = mine.reshape(lanes, -1, width)
    other = other.reshape(lanes, -1, width)
    pair = set_half(core, mine)
    pair = set_half(1 - core, other, pair)
    pair, arrived = lax.optimization_barrier((pair, arrived))
    branch_keys = arrived.reshape(1, replicas, slots_each, part)
    rollout_weights = pair.reshape(2 * chips * rows, width)
    return (new_master, new_moment, new_second, rollout_weights, branch_keys)


def solution(mesh):
    size = mesh.shape
    mesh = Mesh(
        mesh.devices.reshape(2, 2, 4, 2, size["tp"]), ("xlo", "core", "y", "xhi", "tp")
    )
    shard = P(("tp",) + PLANE, None)
    return jax.shard_map(
        local,
        mesh=mesh,
        in_specs=(shard, shard, shard, shard, P(), P("tp", None), P(PLANE, "tp"), P(PLANE, None)),
        out_specs=(shard, shard, shard, P("tp", None), P(PLANE, None, None, "tp")),
        check_vma=False,
    )
```

```python
import functools

import jax
import jax.numpy as jnp
from jax import lax
from jax.experimental import pallas as pl
from jax.experimental.pallas import tpu as pltpu
from jax.sharding import Mesh
from jax.sharding import PartitionSpec as P

learn_rate = 0.05
decay_rate = 0.1

PLANE = ("xlo", "core", "y", "xhi")
CHIPS = ("xlo", "y", "xhi")
LEVELS = 32767.0
TAIL = 16
PIECES = 2
CHUNKS = 4
MOST_STEPS = 8


def coded(value):
    top = jnp.maximum(jnp.max(jnp.abs(value), axis=0, keepdims=True), 1.2e-38)
    power = jnp.ceil(jnp.log(top) * (256.0 / 0.6931471805599453) + 0.01)
    power = jnp.clip(power, -32256.0, 32256.0)
    scaled = value * jnp.exp2(power * (-1.0 / 256.0)) * LEVELS
    codes = jnp.clip(jnp.round(scaled), -LEVELS, LEVELS)
    tail = jnp.broadcast_to(power, (TAIL, value.shape[1]))
    return codes.astype(jnp.int32).astype(jnp.int16), tail.astype(jnp.int32).astype(jnp.int16)


def put_coded(ref, value):
    codes, tail = coded(value)
    rows = value.shape[0]
    ref[0:rows, :] = codes
    ref[rows : rows + TAIL, :] = tail


def take_coded(ref):
    rows = ref.shape[0] - TAIL
    power = ref[rows : rows + TAIL, :].astype(jnp.int32).astype(jnp.float32)[0:1, :]
    codes = ref[0:rows, :].astype(jnp.int32).astype(jnp.float32)
    return codes * (1.0 / LEVELS) * jnp.exp2(power * (1.0 / 256.0))


def update_kernel(
    step_h, master_h, moment_h, second_h, gradient_h,
    new_master_h, new_moment_h, new_second_h, spread_h,
    step, master, moment, second, gradient, new_master, new_moment, new_second, fresh,
    step_sem, sems, out_sems, spread_sems,
):
    sources = [moment_h, gradient_h, second_h, master_h]
    places = [moment, gradient, second, master]
    rows = master.shape[0] // PIECES
    pieces = [pl.ds(p * rows, rows) for p in range(PIECES)]
    load_step = pltpu.make_async_copy(step_h, step, step_sem)
    load_step.start()
    loads = [
        [
            pltpu.make_async_copy(source.at[piece], place.at[piece], sems.at[p, k])
            for k, (source, place) in enumerate(zip(sources, places))
        ]
        for p, piece in enumerate(pieces)
    ]
    for group in loads:
        for load in group:
            load.start()

    load_step.wait()
    steps = jnp.broadcast_to(step[...], (1, master.shape[1]))
    first = other = jnp.ones(steps.shape, jnp.float32)
    for k in range(MOST_STEPS):
        first = jnp.where(steps > k, first * 0.9, first)
        other = jnp.where(steps > k, other * 0.95, other)
    first_fix, second_fix = 1.0 - first, 1.0 - other
    finished = [(new_master, new_master_h), (new_moment, new_moment_h), (new_second, new_second_h)]
    stores = []
    for p, piece in enumerate(pieces):
        for load in loads[p]:
            load.wait()
        g, old = gradient[piece, :], master[piece, :]
        m = 0.9 * moment[piece, :] + 0.1 * g
        v = 0.95 * second[piece, :] + 0.05 * g * g
        update = m / first_fix / (jnp.sqrt(v / second_fix) + 1e-08)
        new = old - learn_rate * (update + decay_rate * old)
        fresh[piece, :] = new.astype(jnp.bfloat16)
        new_moment[piece, :] = m
        new_second[piece, :] = v
        new_master[piece, :] = new
        group = [
            pltpu.make_async_copy(fresh.at[piece], spread_h.at[k, piece], spread_sems.at[p, k])
            for k in range(spread_h.shape[0])
        ]
        group += [
            pltpu.make_async_copy(source.at[piece], place.at[piece], out_sems.at[p, k])
            for k, (source, place) in enumerate(finished)
        ]
        for store in group:
            store.start()
        stores += group
    for store in stores:
        store.wait()


def updated(step_count, master, moment, second, gradient, chips):
    anywhere = pl.BlockSpec(memory_space=pl.ANY)
    shard = master.shape
    outs = [jax.ShapeDtypeStruct(shard, jnp.float32)] * 3
    outs += [jax.ShapeDtypeStruct((chips,) + shard, jnp.bfloat16)]
    return pl.pallas_call(
        update_kernel,
        out_shape=outs,
        in_specs=[anywhere] * 5,
        out_specs=[anywhere] * 4,
        scratch_shapes=[pltpu.VMEM((1, 1), jnp.int32)]
        + [pltpu.VMEM(shard, jnp.float32)] * 7
        + [
            pltpu.VMEM(shard, jnp.bfloat16),
            pltpu.SemaphoreType.DMA,
            pltpu.SemaphoreType.DMA((PIECES, 4)),
            pltpu.SemaphoreType.DMA((PIECES, 3)),
            pltpu.SemaphoreType.DMA((PIECES, chips)),
        ],
        compiler_params=pltpu.CompilerParams(vmem_limit_bytes=60 * 2**20),
        cost_estimate=pl.CostEstimate(
            flops=30 * master.size, bytes_accessed=60 * master.size, transcendentals=3 * master.size
        ),
    )(step_count.reshape(1, 1), master, moment, second, gradient)


def loading(steps, groups, kernel, me, x_h, w_h, *refs):
    x, w, totals, x_sems, w_sems = refs[-5:]
    part = w.shape[2]
    depth = x.shape[1] // CHUNKS
    loads = []
    for c in range(CHUNKS):
        chunk = pl.ds(c * depth, depth)
        group = [pltpu.make_async_copy(x_h.at[:, chunk], x.at[:, chunk], x_sems.at[c])]
        for k, step in enumerate(steps):
            block = lax.rem(me[0] + step, w_h.shape[1] // part)
            columns = pl.ds(pl.multiple_of(block * part, part), part)
            group.append(
                pltpu.make_async_copy(w_h.at[chunk, columns], w.at[k, chunk], w_sems.at[c, k])
            )
        loads.append(group)
        for load in group:
            load.start()
    for c in range(CHUNKS):
        chunk = slice(c * depth, (c + 1) * depth)
        for load in loads[c]:
            load.wait()
        for group in groups:
            columns = jnp.concatenate([w[k, chunk, :] for k in group], axis=1)
            value = jnp.dot(x[:, chunk], columns, preferred_element_type=jnp.float32)
            for i, k in enumerate(group):
                share = value[:, i * part : (i + 1) * part]
                totals[k] = share if c == 0 else totals[k] + share
    kernel(totals, *refs[:-5])


def far_kernel(totals, up, down, far_up, far_down):
    half = totals.shape[1] // 2
    put_coded(up, totals[0])
    put_coded(down, totals[1])
    put_coded(far_up, totals[2, :half])
    put_coded(far_down, totals[2, half:])


def near_kernel(totals, up, down, next_up, next_down, own):
    put_coded(up, totals[0])
    put_coded(down, totals[1])
    next_up[...] = totals[2]
    next_down[...] = totals[3]
    own[...] = totals[4]


def products(kernel, x, w, me, groups, outs):
    rows, depth = x.shape
    steps = [step for group in groups for step in group]
    count = len(steps)
    part = w.shape[1] // 8
    places, at = [], 0
    for group in groups:
        places.append(tuple(range(at, at + len(group))))
        at += len(group)
    anywhere = pl.BlockSpec(memory_space=pl.ANY)
    return pl.pallas_call(
        functools.partial(loading, steps, places, kernel),
        out_shape=outs,
        in_specs=[pl.BlockSpec(memory_space=pltpu.SMEM), anywhere, anywhere],
        out_specs=[pl.BlockSpec(memory_space=pltpu.VMEM)] * len(outs),
        scratch_shapes=[
            pltpu.VMEM((rows, depth), x.dtype),
            pltpu.VMEM((count, depth, part), w.dtype),
            pltpu.VMEM((count, rows, part), jnp.float32),
            pltpu.SemaphoreType.DMA((CHUNKS,)),
            pltpu.SemaphoreType.DMA((CHUNKS, count)),
        ],
        compiler_params=pltpu.CompilerParams(vmem_limit_bytes=52 * 2**20),
        cost_estimate=pl.CostEstimate(
            flops=2 * rows * depth * part * count,
            bytes_accessed=2 * depth * (rows + part * count),
            transcendentals=0,
        ),
    )(me, x, w)


def local_call(kernel, outs, *args, flops=0):
    return pl.pallas_call(
        kernel,
        out_shape=outs,
        compiler_params=pltpu.CompilerParams(vmem_limit_bytes=40 * 2**20),
        cost_estimate=pl.CostEstimate(flops=flops, bytes_accessed=2**20, transcendentals=0),
    )(*args)


def merge_kernel(own_a, next_a, far_a, own_b, next_b, far_b, qa, qb):
    half = own_a.shape[0] // 2
    total = own_a[...] + take_coded(next_a)
    total = jnp.concatenate([total[:half] + take_coded(far_a), total[half:]], axis=0)
    put_coded(qa, total)
    total = own_b[...] + take_coded(next_b)
    total = jnp.concatenate([total[:half], total[half:] + take_coded(far_b)], axis=0)
    put_coded(qb, total)


def selector_kernel(target_ref, out):
    places, rows = out.shape
    replicas = 32
    each = places // replicas
    target = target_ref[...]
    onehot = (lax.broadcasted_iota(jnp.int32, (replicas, rows), 0) == target).astype(jnp.float32)
    before = (
        lax.broadcasted_iota(jnp.int32, (rows, rows), 0)
        < lax.broadcasted_iota(jnp.int32, (rows, rows), 1)
    ).astype(jnp.bfloat16)
    ranks = jnp.dot(onehot.astype(jnp.bfloat16), before, preferred_element_type=jnp.float32)
    rank = jnp.sum(ranks * onehot, axis=0, keepdims=True).astype(jnp.int32)
    position = target * each + rank
    out[...] = (lax.broadcasted_iota(jnp.int32, (places, rows), 0) == position).astype(jnp.float32).astype(jnp.bfloat16)


def final_kernel(own, ra, rb, rc, rd, selector, out):
    keys = own[...] + take_coded(ra) + take_coded(rb) + take_coded(rc) + take_coded(rd)
    out[...] = jnp.dot(
        selector[...], keys.astype(jnp.bfloat16), preferred_element_type=jnp.float32
    ).astype(jnp.bfloat16)


def half_kernel(place, half, *refs):
    refs[-1][...] = half[...].reshape(refs[-1].shape)


def set_half(place, half, pair=None):
    lanes, rows, width = half.shape
    step = rows // 2
    args = (place, half) + (() if pair is None else (pair,))
    return pl.pallas_call(
        half_kernel,
        out_shape=jax.ShapeDtypeStruct((lanes, 2, rows, width), half.dtype),
        grid_spec=pltpu.PrefetchScalarGridSpec(
            num_scalar_prefetch=1,
            grid=(lanes, rows // step),
            in_specs=[pl.BlockSpec((1, step, width), lambda i, j, place: (i, j, 0))]
            + [pl.BlockSpec(memory_space=pl.ANY)] * (len(args) - 2),
            out_specs=pl.BlockSpec((1, 1, step, width), lambda i, j, place: (i, place[0], j, 0)),
        ),
        input_output_aliases={} if pair is None else {2: 0},
        compiler_params=pltpu.CompilerParams(vmem_limit_bytes=16 * 2**20),
        cost_estimate=pl.CostEstimate(flops=0, bytes_accessed=4 * half.size, transcendentals=0),
    )(*args)


def along_tp(value, step):
    size = lax.axis_size("tp")
    return lax.ppermute(value, "tp", [(i, (i + step) % size) for i in range(size)])


def local(master, moment, second, gradient, step_count, old_weights, branch_rows, assignment):
    rows, width = master.shape
    chips = lax.axis_size(CHIPS)
    size = lax.axis_size("tp")
    me = jnp.reshape(lax.axis_index("tp"), (1,)).astype(jnp.int32)
    count = branch_rows.shape[0]
    part = old_weights.shape[1] // size
    code = lambda n: jax.ShapeDtypeStruct((n + TAIL, part), jnp.int16)
    full = jax.ShapeDtypeStruct((count, part), jnp.float32)
    new_master, new_moment, new_second, spread = updated(
        step_count, master, moment, second, gradient, chips
    )
    mine = lax.all_to_all(spread, CHIPS, split_axis=0, concat_axis=0, tiled=True)
    q3, q5, q4a, q4b = products(
        far_kernel, branch_rows, old_weights, me, ((3, 5), (4,)),
        [code(count), code(count), code(count // 2), code(count // 2)],
    )
    r3, r5 = along_tp(q3, 1), along_tp(q5, -1)
    r4a, r4b = along_tp(q4a, 2), along_tp(q4b, -2)
    q1, q7, p2, p6, p0 = products(
        near_kernel, branch_rows, old_weights, me, ((1, 7), (2, 6), (0,)),
        [code(count), code(count), full, full, full],
    )
    r1, r7 = along_tp(q1, 1), along_tp(q7, -1)
    q2, q6 = local_call(merge_kernel, [code(count), code(count)], p2, r3, r4a, p6, r5, r4b)
    r2, r6 = along_tp(q2, 2), along_tp(q6, -2)
    replicas = lax.axis_size(PLANE)
    slots_each = 2 * count // replicas
    places = replicas * slots_each
    selector = local_call(
        selector_kernel, jax.ShapeDtypeStruct((places, count), jnp.bfloat16), assignment.reshape(1, count)
    )
    mine = lax.optimization_barrier((mine, r1, r7, r2, r6))[0]
    placed = local_call(
        final_kernel, jax.ShapeDtypeStruct((places, part), jnp.bfloat16), p0, r1, r7, r2, r6, selector
    )
    placed = placed.reshape(replicas, slots_each, part)
    arrived = lax.all_to_all(placed, PLANE, split_axis=0, concat_axis=0, tiled=True)
    other = lax.ppermute(mine, "core", [(0, 1), (1, 0)])
    core = jnp.reshape(lax.axis_index("core"), (1,)).astype(jnp.int32)
    lanes = lax.axis_size("xlo")
    mine = mine.reshape(lanes, -1, width)
    other = other.reshape(lanes, -1, width)
    pair = set_half(core, mine)
    pair = set_half(1 - core, other, pair)
    pair, arrived = lax.optimization_barrier((pair, arrived))
    branch_keys = arrived.reshape(1, replicas, slots_each, part)
    rollout_weights = pair.reshape(2 * chips * rows, width)
    return (new_master, new_moment, new_second, rollout_weights, branch_keys)


def solution(mesh):
    size = mesh.shape
    mesh = Mesh(
        mesh.devices.reshape(2, 2, 4, 2, size["tp"]), ("xlo", "core", "y", "xhi", "tp")
    )
    shard = P(("tp",) + PLANE, None)
    return jax.shard_map(
        local,
        mesh=mesh,
        in_specs=(shard, shard, shard, shard, P(), P("tp", None), P(PLANE, "tp"), P(PLANE, None)),
        out_specs=(shard, shard, shard, P("tp", None), P(PLANE, None, None, "tp")),
        check_vma=False,
    )
```

```python
import functools

import jax
import jax.numpy as jnp
from jax import lax
from jax.experimental import pallas as pl
from jax.experimental.pallas import tpu as pltpu
from jax.sharding import Mesh
from jax.sharding import PartitionSpec as P

learn_rate = 0.05
decay_rate = 0.1

PLANE = ("xlo", "core", "y", "xhi")
CHIPS = ("xlo", "y", "xhi")
LEVELS = 32767.0
TAIL = 16
PIECES = 2
CHUNKS = 4
MOST_STEPS = 8


def coded(value):
    top = jnp.maximum(jnp.max(jnp.abs(value), axis=0, keepdims=True), 1.2e-38)
    power = jnp.ceil(jnp.log(top) * (256.0 / 0.6931471805599453) + 0.01)
    power = jnp.clip(power, -32256.0, 32256.0)
    scaled = value * jnp.exp2(power * (-1.0 / 256.0)) * LEVELS
    codes = jnp.clip(jnp.round(scaled), -LEVELS, LEVELS)
    tail = jnp.broadcast_to(power, (TAIL, value.shape[1]))
    return codes.astype(jnp.int32).astype(jnp.int16), tail.astype(jnp.int32).astype(jnp.int16)


def put_coded(ref, value):
    codes, tail = coded(value)
    rows = value.shape[0]
    ref[0:rows, :] = codes
    ref[rows : rows + TAIL, :] = tail


def take_coded(ref):
    rows = ref.shape[0] - TAIL
    power = ref[rows : rows + TAIL, :].astype(jnp.int32).astype(jnp.float32)[0:1, :]
    codes = ref[0:rows, :].astype(jnp.int32).astype(jnp.float32)
    return codes * (1.0 / LEVELS) * jnp.exp2(power * (1.0 / 256.0))


def update_kernel(
    step_h, master_h, moment_h, second_h, gradient_h,
    new_master_h, new_moment_h, new_second_h, spread_h,
    step, master, moment, second, gradient, new_master, new_moment, new_second, fresh,
    step_sem, sems, out_sems, spread_sems,
):
    sources = [moment_h, gradient_h, second_h, master_h]
    places = [moment, gradient, second, master]
    rows = master.shape[0] // PIECES
    pieces = [pl.ds(p * rows, rows) for p in range(PIECES)]
    load_step = pltpu.make_async_copy(step_h, step, step_sem)
    load_step.start()
    loads = [
        [
            pltpu.make_async_copy(source.at[piece], place.at[piece], sems.at[p, k])
            for k, (source, place) in enumerate(zip(sources, places))
        ]
        for p, piece in enumerate(pieces)
    ]
    for group in loads:
        for load in group:
            load.start()

    load_step.wait()
    steps = jnp.broadcast_to(step[...], (1, master.shape[1]))
    first = other = jnp.ones(steps.shape, jnp.float32)
    for k in range(MOST_STEPS):
        first = jnp.where(steps > k, first * 0.9, first)
        other = jnp.where(steps > k, other * 0.95, other)
    first_fix, second_fix = 1.0 - first, 1.0 - other
    finished = [(new_master, new_master_h), (new_moment, new_moment_h), (new_second, new_second_h)]
    stores = []
    for p, piece in enumerate(pieces):
        for load in loads[p]:
            load.wait()
        g, old = gradient[piece, :], master[piece, :]
        m = 0.9 * moment[piece, :] + 0.1 * g
        v = 0.95 * second[piece, :] + 0.05 * g * g
        update = m / first_fix / (jnp.sqrt(v / second_fix) + 1e-08)
        new = old - learn_rate * (update + decay_rate * old)
        fresh[piece, :] = new.astype(jnp.bfloat16)
        new_moment[piece, :] = m
        new_second[piece, :] = v
        new_master[piece, :] = new
        group = [
            pltpu.make_async_copy(fresh.at[piece], spread_h.at[k, piece], spread_sems.at[p, k])
            for k in range(spread_h.shape[0])
        ]
        group += [
            pltpu.make_async_copy(source.at[piece], place.at[piece], out_sems.at[p, k])
            for k, (source, place) in enumerate(finished)
        ]
        for store in group:
            store.start()
        stores += group
    for store in stores:
        store.wait()


def updated(step_count, master, moment, second, gradient, chips):
    anywhere = pl.BlockSpec(memory_space=pl.ANY)
    shard = master.shape
    outs = [jax.ShapeDtypeStruct(shard, jnp.float32)] * 3
    outs += [jax.ShapeDtypeStruct((chips,) + shard, jnp.bfloat16)]
    return pl.pallas_call(
        update_kernel,
        out_shape=outs,
        in_specs=[anywhere] * 5,
        out_specs=[anywhere] * 4,
        scratch_shapes=[pltpu.VMEM((1, 1), jnp.int32)]
        + [pltpu.VMEM(shard, jnp.float32)] * 7
        + [
            pltpu.VMEM(shard, jnp.bfloat16),
            pltpu.SemaphoreType.DMA,
            pltpu.SemaphoreType.DMA((PIECES, 4)),
            pltpu.SemaphoreType.DMA((PIECES, 3)),
            pltpu.SemaphoreType.DMA((PIECES, chips)),
        ],
        compiler_params=pltpu.CompilerParams(vmem_limit_bytes=60 * 2**20),
        cost_estimate=pl.CostEstimate(
            flops=30 * master.size, bytes_accessed=60 * master.size, transcendentals=3 * master.size
        ),
    )(step_count.reshape(1, 1), master, moment, second, gradient)


def loading(steps, groups, kernel, me, x_h, w_h, *refs):
    x, w, totals, x_sems, w_sems = refs[-5:]
    part = w.shape[2]
    depth = x.shape[1] // CHUNKS
    loads = []
    for c in range(CHUNKS):
        chunk = pl.ds(c * depth, depth)
        group = [pltpu.make_async_copy(x_h.at[:, chunk], x.at[:, chunk], x_sems.at[c])]
        for k, step in enumerate(steps):
            block = lax.rem(me[0] + step, w_h.shape[1] // part)
            columns = pl.ds(pl.multiple_of(block * part, part), part)
            group.append(
                pltpu.make_async_copy(w_h.at[chunk, columns], w.at[k, chunk], w_sems.at[c, k])
            )
        loads.append(group)
        for load in group:
            load.start()
    for c in range(CHUNKS):
        chunk = slice(c * depth, (c + 1) * depth)
        for load in loads[c]:
            load.wait()
        for group in groups:
            columns = jnp.concatenate([w[k, chunk, :] for k in group], axis=1)
            value = jnp.dot(x[:, chunk], columns, preferred_element_type=jnp.float32)
            for i, k in enumerate(group):
                share = value[:, i * part : (i + 1) * part]
                totals[k] = share if c == 0 else totals[k] + share
    kernel(totals, *refs[:-5])


def products_kernel(totals, up, down, far_up, far_down, next_up, next_down, two_up, two_down, own):
    half = totals.shape[1] // 2
    put_coded(up, totals[0])
    put_coded(down, totals[1])
    put_coded(far_up, totals[2, :half])
    put_coded(far_down, totals[2, half:])
    own[...] = totals[3]
    two_up[...] = totals[4]
    two_down[...] = totals[5]
    put_coded(next_up, totals[6])
    put_coded(next_down, totals[7])


def products(kernel, x, w, me, groups, outs):
    rows, depth = x.shape
    steps = [step for group in groups for step in group]
    count = len(steps)
    part = w.shape[1] // 8
    places, at = [], 0
    for group in groups:
        places.append(tuple(range(at, at + len(group))))
        at += len(group)
    anywhere = pl.BlockSpec(memory_space=pl.ANY)
    return pl.pallas_call(
        functools.partial(loading, steps, places, kernel),
        out_shape=outs,
        in_specs=[pl.BlockSpec(memory_space=pltpu.SMEM), anywhere, anywhere],
        out_specs=[pl.BlockSpec(memory_space=pltpu.VMEM)] * len(outs),
        scratch_shapes=[
            pltpu.VMEM((rows, depth), x.dtype),
            pltpu.VMEM((count, depth, part), w.dtype),
            pltpu.VMEM((count, rows, part), jnp.float32),
            pltpu.SemaphoreType.DMA((CHUNKS,)),
            pltpu.SemaphoreType.DMA((CHUNKS, count)),
        ],
        compiler_params=pltpu.CompilerParams(vmem_limit_bytes=52 * 2**20),
        cost_estimate=pl.CostEstimate(
            flops=2 * rows * depth * part * count,
            bytes_accessed=2 * depth * (rows + part * count),
            transcendentals=0,
        ),
    )(me, x, w)


def local_call(kernel, outs, *args, flops=0):
    return pl.pallas_call(
        kernel,
        out_shape=outs,
        compiler_params=pltpu.CompilerParams(vmem_limit_bytes=40 * 2**20),
        cost_estimate=pl.CostEstimate(flops=flops, bytes_accessed=2**20, transcendentals=0),
    )(*args)


def merge_kernel(own_a, next_a, far_a, own_b, next_b, far_b, qa, qb):
    half = own_a.shape[0] // 2
    total = own_a[...] + take_coded(next_a)
    total = jnp.concatenate([total[:half] + take_coded(far_a), total[half:]], axis=0)
    put_coded(qa, total)
    total = own_b[...] + take_coded(next_b)
    total = jnp.concatenate([total[:half], total[half:] + take_coded(far_b)], axis=0)
    put_coded(qb, total)


def selector_kernel(target_ref, out):
    places, rows = out.shape
    replicas = 32
    each = places // replicas
    target = target_ref[...]
    onehot = (lax.broadcasted_iota(jnp.int32, (replicas, rows), 0) == target).astype(jnp.float32)
    before = (
        lax.broadcasted_iota(jnp.int32, (rows, rows), 0)
        < lax.broadcasted_iota(jnp.int32, (rows, rows), 1)
    ).astype(jnp.bfloat16)
    ranks = jnp.dot(onehot.astype(jnp.bfloat16), before, preferred_element_type=jnp.float32)
    rank = jnp.sum(ranks * onehot, axis=0, keepdims=True).astype(jnp.int32)
    position = target * each + rank
    out[...] = (lax.broadcasted_iota(jnp.int32, (places, rows), 0) == position).astype(jnp.float32).astype(jnp.bfloat16)


def final_kernel(own, ra, rb, rc, rd, selector, out):
    keys = own[...] + take_coded(ra) + take_coded(rb) + take_coded(rc) + take_coded(rd)
    out[...] = jnp.dot(
        selector[...], keys.astype(jnp.bfloat16), preferred_element_type=jnp.float32
    ).astype(jnp.bfloat16)


def half_kernel(place, half, *refs):
    refs[-1][...] = half[...].reshape(refs[-1].shape)


def set_half(place, half, pair=None):
    lanes, rows, width = half.shape
    step = rows // 2
    args = (place, half) + (() if pair is None else (pair,))
    return pl.pallas_call(
        half_kernel,
        out_shape=jax.ShapeDtypeStruct((lanes, 2, rows, width), half.dtype),
        grid_spec=pltpu.PrefetchScalarGridSpec(
            num_scalar_prefetch=1,
            grid=(lanes, rows // step),
            in_specs=[pl.BlockSpec((1, step, width), lambda i, j, place: (i, j, 0))]
            + [pl.BlockSpec(memory_space=pl.ANY)] * (len(args) - 2),
            out_specs=pl.BlockSpec((1, 1, step, width), lambda i, j, place: (i, place[0], j, 0)),
        ),
        input_output_aliases={} if pair is None else {2: 0},
        compiler_params=pltpu.CompilerParams(vmem_limit_bytes=16 * 2**20),
        cost_estimate=pl.CostEstimate(flops=0, bytes_accessed=4 * half.size, transcendentals=0),
    )(*args)


def along_tp(value, step):
    size = lax.axis_size("tp")
    return lax.ppermute(value, "tp", [(i, (i + step) % size) for i in range(size)])


def local(master, moment, second, gradient, step_count, old_weights, branch_rows, assignment):
    rows, width = master.shape
    chips = lax.axis_size(CHIPS)
    size = lax.axis_size("tp")
    me = jnp.reshape(lax.axis_index("tp"), (1,)).astype(jnp.int32)
    count = branch_rows.shape[0]
    part = old_weights.shape[1] // size
    code = lambda n: jax.ShapeDtypeStruct((n + TAIL, part), jnp.int16)
    full = jax.ShapeDtypeStruct((count, part), jnp.float32)
    new_master, new_moment, new_second, spread = updated(
        step_count, master, moment, second, gradient, chips
    )
    mine = lax.all_to_all(spread, CHIPS, split_axis=0, concat_axis=0, tiled=True)
    q3, q5, q4a, q4b, q1, q7, p2, p6, p0 = products(
        products_kernel, branch_rows, old_weights, me, ((3, 5), (4, 0), (2, 6), (1, 7)),
        [code(count)] * 2 + [code(count // 2)] * 2 + [code(count)] * 2 + [full] * 3,
    )
    r3, r5 = along_tp(q3, 1), along_tp(q5, -1)
    r4a, r4b = along_tp(q4a, 2), along_tp(q4b, -2)
    r1, r7 = along_tp(q1, 1), along_tp(q7, -1)
    q2, q6 = local_call(merge_kernel, [code(count), code(count)], p2, r3, r4a, p6, r5, r4b)
    r2, r6 = along_tp(q2, 2), along_tp(q6, -2)
    replicas = lax.axis_size(PLANE)
    slots_each = 2 * count // replicas
    places = replicas * slots_each
    selector = local_call(
        selector_kernel, jax.ShapeDtypeStruct((places, count), jnp.bfloat16), assignment.reshape(1, count)
    )
    placed = local_call(
        final_kernel, jax.ShapeDtypeStruct((places, part), jnp.bfloat16), p0, r1, r7, r2, r6, selector
    )
    mine = lax.optimization_barrier((mine, placed))[0]
    placed = placed.reshape(replicas, slots_each, part)
    arrived = lax.all_to_all(placed, PLANE, split_axis=0, concat_axis=0, tiled=True)
    other = lax.ppermute(mine, "core", [(0, 1), (1, 0)])
    core = jnp.reshape(lax.axis_index("core"), (1,)).astype(jnp.int32)
    lanes = lax.axis_size("xlo")
    mine = mine.reshape(lanes, -1, width)
    other = other.reshape(lanes, -1, width)
    pair = set_half(core, mine)
    pair = set_half(1 - core, other, pair)
    pair, arrived = lax.optimization_barrier((pair, arrived))
    branch_keys = arrived.reshape(1, replicas, slots_each, part)
    rollout_weights = pair.reshape(2 * chips * rows, width)
    return (new_master, new_moment, new_second, rollout_weights, branch_keys)


def solution(mesh):
    size = mesh.shape
    mesh = Mesh(
        mesh.devices.reshape(2, 2, 4, 2, size["tp"]), ("xlo", "core", "y", "xhi", "tp")
    )
    shard = P(("tp",) + PLANE, None)
    return jax.shard_map(
        local,
        mesh=mesh,
        in_specs=(shard, shard, shard, shard, P(), P("tp", None), P(PLANE, "tp"), P(PLANE, None)),
        out_specs=(shard, shard, shard, P("tp", None), P(PLANE, None, None, "tp")),
        check_vma=False,
    )
```

```python
import functools

import jax
import jax.numpy as jnp
from jax import lax
from jax.experimental import pallas as pl
from jax.experimental.pallas import tpu as pltpu
from jax.sharding import Mesh
from jax.sharding import PartitionSpec as P

learn_rate = 0.05
decay_rate = 0.1

PLANE = ("xlo", "core", "y", "xhi")
CHIPS = ("xlo", "y", "xhi")
LEVELS = 32767.0
TAIL = 16
PIECES = 2
CHUNKS = 4
MOST_STEPS = 8


def coded(value):
    top = jnp.maximum(jnp.max(jnp.abs(value), axis=0, keepdims=True), 1.2e-38)
    power = jnp.ceil(jnp.log(top) * (256.0 / 0.6931471805599453) + 0.01)
    power = jnp.clip(power, -32256.0, 32256.0)
    scaled = value * jnp.exp2(power * (-1.0 / 256.0)) * LEVELS
    codes = jnp.clip(jnp.round(scaled), -LEVELS, LEVELS)
    tail = jnp.broadcast_to(power, (TAIL, value.shape[1]))
    return codes.astype(jnp.int32).astype(jnp.int16), tail.astype(jnp.int32).astype(jnp.int16)


def put_coded(ref, value):
    codes, tail = coded(value)
    rows = value.shape[0]
    ref[0:rows, :] = codes
    ref[rows : rows + TAIL, :] = tail


def take_coded(ref):
    rows = ref.shape[0] - TAIL
    power = ref[rows : rows + TAIL, :].astype(jnp.int32).astype(jnp.float32)[0:1, :]
    codes = ref[0:rows, :].astype(jnp.int32).astype(jnp.float32)
    return codes * (1.0 / LEVELS) * jnp.exp2(power * (1.0 / 256.0))


def update_kernel(
    step_h, master_h, moment_h, second_h, gradient_h,
    new_master_h, new_moment_h, new_second_h, spread_h,
    step, master, moment, second, gradient, new_master, new_moment, new_second, fresh,
    step_sem, sems, out_sems, spread_sems,
):
    sources = [moment_h, gradient_h, second_h, master_h]
    places = [moment, gradient, second, master]
    rows = master.shape[0] // PIECES
    pieces = [pl.ds(p * rows, rows) for p in range(PIECES)]
    load_step = pltpu.make_async_copy(step_h, step, step_sem)
    load_step.start()
    loads = [
        [
            pltpu.make_async_copy(source.at[piece], place.at[piece], sems.at[p, k])
            for k, (source, place) in enumerate(zip(sources, places))
        ]
        for p, piece in enumerate(pieces)
    ]
    for group in loads:
        for load in group:
            load.start()

    load_step.wait()
    steps = jnp.broadcast_to(step[...], (1, master.shape[1]))
    first = other = jnp.ones(steps.shape, jnp.float32)
    for k in range(MOST_STEPS):
        first = jnp.where(steps > k, first * 0.9, first)
        other = jnp.where(steps > k, other * 0.95, other)
    first_fix, second_fix = 1.0 - first, 1.0 - other
    finished = [(new_master, new_master_h), (new_moment, new_moment_h), (new_second, new_second_h)]
    stores = []
    for p, piece in enumerate(pieces):
        for load in loads[p]:
            load.wait()
        g, old = gradient[piece, :], master[piece, :]
        m = 0.9 * moment[piece, :] + 0.1 * g
        v = 0.95 * second[piece, :] + 0.05 * g * g
        update = m / first_fix / (jnp.sqrt(v / second_fix) + 1e-08)
        new = old - learn_rate * (update + decay_rate * old)
        fresh[piece, :] = new.astype(jnp.bfloat16)
        new_moment[piece, :] = m
        new_second[piece, :] = v
        new_master[piece, :] = new
        group = [
            pltpu.make_async_copy(fresh.at[piece], spread_h.at[k, piece], spread_sems.at[p, k])
            for k in range(spread_h.shape[0])
        ]
        group += [
            pltpu.make_async_copy(source.at[piece], place.at[piece], out_sems.at[p, k])
            for k, (source, place) in enumerate(finished)
        ]
        for store in group:
            store.start()
        stores += group
    for store in stores:
        store.wait()


def updated(step_count, master, moment, second, gradient, chips):
    anywhere = pl.BlockSpec(memory_space=pl.ANY)
    shard = master.shape
    outs = [jax.ShapeDtypeStruct(shard, jnp.float32)] * 3
    outs += [jax.ShapeDtypeStruct((chips,) + shard, jnp.bfloat16)]
    return pl.pallas_call(
        update_kernel,
        out_shape=outs,
        in_specs=[anywhere] * 5,
        out_specs=[anywhere] * 4,
        scratch_shapes=[pltpu.VMEM((1, 1), jnp.int32)]
        + [pltpu.VMEM(shard, jnp.float32)] * 7
        + [
            pltpu.VMEM(shard, jnp.bfloat16),
            pltpu.SemaphoreType.DMA,
            pltpu.SemaphoreType.DMA((PIECES, 4)),
            pltpu.SemaphoreType.DMA((PIECES, 3)),
            pltpu.SemaphoreType.DMA((PIECES, chips)),
        ],
        compiler_params=pltpu.CompilerParams(vmem_limit_bytes=60 * 2**20),
        cost_estimate=pl.CostEstimate(
            flops=30 * master.size, bytes_accessed=60 * master.size, transcendentals=3 * master.size
        ),
    )(step_count.reshape(1, 1), master, moment, second, gradient)


def loading(steps, groups, kernel, me, x_h, w_h, *refs):
    x, w, totals, x_sems, w_sems = refs[-5:]
    part = totals.shape[2]
    blocks = [lax.rem(me[0] + step, len(steps)) * part for step in steps]
    depth = x.shape[1] // CHUNKS
    loads = []
    for c in range(CHUNKS):
        chunk = pl.ds(c * depth, depth)
        group = [
            pltpu.make_async_copy(x_h.at[:, chunk], x.at[:, chunk], x_sems.at[c]),
            pltpu.make_async_copy(w_h.at[chunk], w.at[chunk], w_sems.at[c]),
        ]
        loads.append(group)
        for load in group:
            load.start()
    for c in range(CHUNKS):
        chunk = slice(c * depth, (c + 1) * depth)
        for load in loads[c]:
            load.wait()
        for group in groups:
            columns = jnp.concatenate(
                [w[chunk, pl.ds(pl.multiple_of(blocks[k], part), part)] for k in group], axis=1
            )
            value = jnp.dot(x[:, chunk], columns, preferred_element_type=jnp.float32)
            for i, k in enumerate(group):
                share = value[:, i * part : (i + 1) * part]
                totals[k] = share if c == 0 else totals[k] + share
    kernel(totals, *refs[:-5])


def products_kernel(totals, up, down, far_up, far_down, next_up, next_down, two_up, two_down, own):
    half = totals.shape[1] // 2
    put_coded(up, totals[0])
    put_coded(down, totals[1])
    put_coded(far_up, totals[2, :half])
    put_coded(far_down, totals[2, half:])
    own[...] = totals[3]
    two_up[...] = totals[4]
    two_down[...] = totals[5]
    put_coded(next_up, totals[6])
    put_coded(next_down, totals[7])


def products(kernel, x, w, me, groups, outs):
    rows, depth = x.shape
    steps = [step for group in groups for step in group]
    count = len(steps)
    part = w.shape[1] // 8
    places, at = [], 0
    for group in groups:
        places.append(tuple(range(at, at + len(group))))
        at += len(group)
    anywhere = pl.BlockSpec(memory_space=pl.ANY)
    return pl.pallas_call(
        functools.partial(loading, steps, places, kernel),
        out_shape=outs,
        in_specs=[pl.BlockSpec(memory_space=pltpu.SMEM), anywhere, anywhere],
        out_specs=[pl.BlockSpec(memory_space=pltpu.VMEM)] * len(outs),
        scratch_shapes=[
            pltpu.VMEM((rows, depth), x.dtype),
            pltpu.VMEM(w.shape, w.dtype),
            pltpu.VMEM((count, rows, part), jnp.float32),
            pltpu.SemaphoreType.DMA((CHUNKS,)),
            pltpu.SemaphoreType.DMA((CHUNKS,)),
        ],
        compiler_params=pltpu.CompilerParams(vmem_limit_bytes=52 * 2**20),
        cost_estimate=pl.CostEstimate(
            flops=2 * rows * depth * part * count,
            bytes_accessed=2 * depth * (rows + part * count),
            transcendentals=0,
        ),
    )(me, x, w)


def local_call(kernel, outs, *args, flops=0):
    return pl.pallas_call(
        kernel,
        out_shape=outs,
        compiler_params=pltpu.CompilerParams(vmem_limit_bytes=40 * 2**20),
        cost_estimate=pl.CostEstimate(flops=flops, bytes_accessed=2**20, transcendentals=0),
    )(*args)


def merge_kernel(own_a, next_a, far_a, own_b, next_b, far_b, qa, qb):
    half = own_a.shape[0] // 2
    total = own_a[...] + take_coded(next_a)
    total = jnp.concatenate([total[:half] + take_coded(far_a), total[half:]], axis=0)
    put_coded(qa, total)
    total = own_b[...] + take_coded(next_b)
    total = jnp.concatenate([total[:half], total[half:] + take_coded(far_b)], axis=0)
    put_coded(qb, total)


def selector_kernel(target_ref, out):
    places, rows = out.shape
    replicas = 32
    each = places // replicas
    target = target_ref[...]
    onehot = (lax.broadcasted_iota(jnp.int32, (replicas, rows), 0) == target).astype(jnp.float32)
    before = (
        lax.broadcasted_iota(jnp.int32, (rows, rows), 0)
        < lax.broadcasted_iota(jnp.int32, (rows, rows), 1)
    ).astype(jnp.bfloat16)
    ranks = jnp.dot(onehot.astype(jnp.bfloat16), before, preferred_element_type=jnp.float32)
    rank = jnp.sum(ranks * onehot, axis=0, keepdims=True).astype(jnp.int32)
    position = target * each + rank
    out[...] = (lax.broadcasted_iota(jnp.int32, (places, rows), 0) == position).astype(jnp.float32).astype(jnp.bfloat16)


def final_kernel(own, ra, rb, rc, rd, selector, out):
    keys = own[...] + take_coded(ra) + take_coded(rb) + take_coded(rc) + take_coded(rd)
    out[...] = jnp.dot(
        selector[...], keys.astype(jnp.bfloat16), preferred_element_type=jnp.float32
    ).astype(jnp.bfloat16)


def half_kernel(place, half, *refs):
    refs[-1][...] = half[...].reshape(refs[-1].shape)


def set_half(place, half, pair=None):
    lanes, rows, width = half.shape
    step = rows // 2
    args = (place, half) + (() if pair is None else (pair,))
    return pl.pallas_call(
        half_kernel,
        out_shape=jax.ShapeDtypeStruct((lanes, 2, rows, width), half.dtype),
        grid_spec=pltpu.PrefetchScalarGridSpec(
            num_scalar_prefetch=1,
            grid=(lanes, rows // step),
            in_specs=[pl.BlockSpec((1, step, width), lambda i, j, place: (i, j, 0))]
            + [pl.BlockSpec(memory_space=pl.ANY)] * (len(args) - 2),
            out_specs=pl.BlockSpec((1, 1, step, width), lambda i, j, place: (i, place[0], j, 0)),
        ),
        input_output_aliases={} if pair is None else {2: 0},
        compiler_params=pltpu.CompilerParams(vmem_limit_bytes=16 * 2**20),
        cost_estimate=pl.CostEstimate(flops=0, bytes_accessed=4 * half.size, transcendentals=0),
    )(*args)


def along_tp(value, step):
    size = lax.axis_size("tp")
    return lax.ppermute(value, "tp", [(i, (i + step) % size) for i in range(size)])


def local(master, moment, second, gradient, step_count, old_weights, branch_rows, assignment):
    rows, width = master.shape
    chips = lax.axis_size(CHIPS)
    size = lax.axis_size("tp")
    me = jnp.reshape(lax.axis_index("tp"), (1,)).astype(jnp.int32)
    count = branch_rows.shape[0]
    part = old_weights.shape[1] // size
    code = lambda n: jax.ShapeDtypeStruct((n + TAIL, part), jnp.int16)
    full = jax.ShapeDtypeStruct((count, part), jnp.float32)
    new_master, new_moment, new_second, spread = updated(
        step_count, master, moment, second, gradient, chips
    )
    mine = lax.all_to_all(spread, CHIPS, split_axis=0, concat_axis=0, tiled=True)
    q3, q5, q4a, q4b, q1, q7, p2, p6, p0 = products(
        products_kernel, branch_rows, old_weights, me, ((3, 5), (4, 0), (2, 6), (1, 7)),
        [code(count)] * 2 + [code(count // 2)] * 2 + [code(count)] * 2 + [full] * 3,
    )
    r3, r5 = along_tp(q3, 1), along_tp(q5, -1)
    r4a, r4b = along_tp(q4a, 2), along_tp(q4b, -2)
    r1, r7 = along_tp(q1, 1), along_tp(q7, -1)
    q2, q6 = local_call(merge_kernel, [code(count), code(count)], p2, r3, r4a, p6, r5, r4b)
    r2, r6 = along_tp(q2, 2), along_tp(q6, -2)
    replicas = lax.axis_size(PLANE)
    slots_each = 2 * count // replicas
    places = replicas * slots_each
    selector = local_call(
        selector_kernel, jax.ShapeDtypeStruct((places, count), jnp.bfloat16), assignment.reshape(1, count)
    )
    placed = local_call(
        final_kernel, jax.ShapeDtypeStruct((places, part), jnp.bfloat16), p0, r1, r7, r2, r6, selector
    )
    mine = lax.optimization_barrier((mine, placed))[0]
    placed = placed.reshape(replicas, slots_each, part)
    arrived = lax.all_to_all(placed, PLANE, split_axis=0, concat_axis=0, tiled=True)
    other = lax.ppermute(mine, "core", [(0, 1), (1, 0)])
    core = jnp.reshape(lax.axis_index("core"), (1,)).astype(jnp.int32)
    lanes = lax.axis_size("xlo")
    mine = mine.reshape(lanes, -1, width)
    other = other.reshape(lanes, -1, width)
    pair = set_half(core, mine)
    pair = set_half(1 - core, other, pair)
    pair, arrived = lax.optimization_barrier((pair, arrived))
    branch_keys = arrived.reshape(1, replicas, slots_each, part)
    rollout_weights = pair.reshape(2 * chips * rows, width)
    return (new_master, new_moment, new_second, rollout_weights, branch_keys)


def solution(mesh):
    size = mesh.shape
    mesh = Mesh(
        mesh.devices.reshape(2, 2, 4, 2, size["tp"]), ("xlo", "core", "y", "xhi", "tp")
    )
    shard = P(("tp",) + PLANE, None)
    return jax.shard_map(
        local,
        mesh=mesh,
        in_specs=(shard, shard, shard, shard, P(), P("tp", None), P(PLANE, "tp"), P(PLANE, None)),
        out_specs=(shard, shard, shard, P("tp", None), P(PLANE, None, None, "tp")),
        check_vma=False,
    )
```

```python
import functools

import jax
import jax.numpy as jnp
from jax import lax
from jax.experimental import pallas as pl
from jax.experimental.pallas import tpu as pltpu
from jax.sharding import Mesh
from jax.sharding import PartitionSpec as P

learn_rate = 0.05
decay_rate = 0.1

PLANE = ("xlo", "core", "y", "xhi")
CHIPS = ("xlo", "y", "xhi")
LEVELS = 32767.0
TAIL = 16
PIECES = 2
CHUNKS = 4
MOST_STEPS = 8


def coded(value):
    top = jnp.maximum(jnp.max(jnp.abs(value), axis=0, keepdims=True), 1.2e-38)
    power = jnp.ceil(jnp.log(top) * (256.0 / 0.6931471805599453) + 0.01)
    power = jnp.clip(power, -32256.0, 32256.0)
    scaled = value * jnp.exp2(power * (-1.0 / 256.0)) * LEVELS
    codes = jnp.clip(jnp.round(scaled), -LEVELS, LEVELS)
    tail = jnp.broadcast_to(power, (TAIL, value.shape[1]))
    return codes.astype(jnp.int32).astype(jnp.int16), tail.astype(jnp.int32).astype(jnp.int16)


def put_coded(ref, value):
    codes, tail = coded(value)
    rows = value.shape[0]
    ref[0:rows, :] = codes
    ref[rows : rows + TAIL, :] = tail


def take_coded(ref):
    rows = ref.shape[0] - TAIL
    power = ref[rows : rows + TAIL, :].astype(jnp.int32).astype(jnp.float32)[0:1, :]
    codes = ref[0:rows, :].astype(jnp.int32).astype(jnp.float32)
    return codes * (1.0 / LEVELS) * jnp.exp2(power * (1.0 / 256.0))


def update_kernel(
    step_h, master_h, moment_h, second_h, gradient_h,
    new_master_h, new_moment_h, new_second_h, spread_h,
    step, master, moment, second, gradient, new_master, new_moment, new_second, fresh,
    step_sem, sems, out_sems, spread_sems,
):
    sources = [moment_h, gradient_h, second_h, master_h]
    places = [moment, gradient, second, master]
    rows = master.shape[0] // PIECES
    pieces = [pl.ds(p * rows, rows) for p in range(PIECES)]
    load_step = pltpu.make_async_copy(step_h, step, step_sem)
    load_step.start()
    loads = [
        [
            pltpu.make_async_copy(source.at[piece], place.at[piece], sems.at[p, k])
            for k, (source, place) in enumerate(zip(sources, places))
        ]
        for p, piece in enumerate(pieces)
    ]
    for group in loads:
        for load in group:
            load.start()

    load_step.wait()
    steps = jnp.broadcast_to(step[...], (1, master.shape[1]))
    first = other = jnp.ones(steps.shape, jnp.float32)
    for k in range(MOST_STEPS):
        first = jnp.where(steps > k, first * 0.9, first)
        other = jnp.where(steps > k, other * 0.95, other)
    first_fix, second_fix = 1.0 - first, 1.0 - other
    finished = [(new_master, new_master_h), (new_moment, new_moment_h), (new_second, new_second_h)]
    stores = []
    for p, piece in enumerate(pieces):
        for load in loads[p]:
            load.wait()
        g, old = gradient[piece, :], master[piece, :]
        m = 0.9 * moment[piece, :] + 0.1 * g
        v = 0.95 * second[piece, :] + 0.05 * g * g
        update = m / first_fix / (jnp.sqrt(v / second_fix) + 1e-08)
        new = old - learn_rate * (update + decay_rate * old)
        fresh[piece, :] = new.astype(jnp.bfloat16)
        new_moment[piece, :] = m
        new_second[piece, :] = v
        new_master[piece, :] = new
        group = [
            pltpu.make_async_copy(fresh.at[piece], spread_h.at[k, piece], spread_sems.at[p, k])
            for k in range(spread_h.shape[0])
        ]
        group += [
            pltpu.make_async_copy(source.at[piece], place.at[piece], out_sems.at[p, k])
            for k, (source, place) in enumerate(finished)
        ]
        for store in group:
            store.start()
        stores += group
    for store in stores:
        store.wait()


def updated(step_count, master, moment, second, gradient, chips):
    anywhere = pl.BlockSpec(memory_space=pl.ANY)
    shard = master.shape
    outs = [jax.ShapeDtypeStruct(shard, jnp.float32)] * 3
    outs += [jax.ShapeDtypeStruct((chips,) + shard, jnp.bfloat16)]
    return pl.pallas_call(
        update_kernel,
        out_shape=outs,
        in_specs=[anywhere] * 5,
        out_specs=[anywhere] * 4,
        scratch_shapes=[pltpu.VMEM((1, 1), jnp.int32)]
        + [pltpu.VMEM(shard, jnp.float32)] * 7
        + [
            pltpu.VMEM(shard, jnp.bfloat16),
            pltpu.SemaphoreType.DMA,
            pltpu.SemaphoreType.DMA((PIECES, 4)),
            pltpu.SemaphoreType.DMA((PIECES, 3)),
            pltpu.SemaphoreType.DMA((PIECES, chips)),
        ],
        compiler_params=pltpu.CompilerParams(vmem_limit_bytes=60 * 2**20),
        cost_estimate=pl.CostEstimate(
            flops=30 * master.size, bytes_accessed=60 * master.size, transcendentals=3 * master.size
        ),
    )(step_count.reshape(1, 1), master, moment, second, gradient)


def loading(steps, groups, kernel, me, x_h, w_h, *refs):
    x, w, totals, x_sems, w_sems = refs[-5:]
    part = totals.shape[2]
    blocks = [lax.rem(me[0] + step, len(steps)) * part for step in steps]
    depth = x.shape[1] // CHUNKS
    loads = []
    for c in range(CHUNKS):
        chunk = pl.ds(c * depth, depth)
        group = [
            pltpu.make_async_copy(x_h.at[:, chunk], x.at[:, chunk], x_sems.at[c]),
            pltpu.make_async_copy(w_h.at[chunk], w.at[chunk], w_sems.at[c]),
        ]
        loads.append(group)
        for load in group:
            load.start()
    for c in range(CHUNKS):
        chunk = slice(c * depth, (c + 1) * depth)
        for load in loads[c]:
            load.wait()
        for group in groups:
            columns = jnp.concatenate(
                [w[chunk, pl.ds(pl.multiple_of(blocks[k], part), part)] for k in group], axis=1
            )
            value = jnp.dot(x[:, chunk], columns, preferred_element_type=jnp.float32)
            for i, k in enumerate(group):
                share = value[:, i * part : (i + 1) * part]
                totals[k] = share if c == 0 else totals[k] + share
    kernel(totals, *refs[:-5])


def products_kernel(totals, up, down, far_up, far_down, two_up, two_down, own):
    half = totals.shape[1] // 2
    put_coded(up.at[0], totals[0])
    put_coded(down.at[0], totals[1])
    put_coded(far_up, totals[2, :half])
    put_coded(far_down, totals[2, half:])
    own[...] = totals[3]
    two_up[...] = totals[4]
    two_down[...] = totals[5]
    put_coded(up.at[1], totals[6])
    put_coded(down.at[1], totals[7])


def products(kernel, x, w, me, groups, outs):
    rows, depth = x.shape
    steps = [step for group in groups for step in group]
    count = len(steps)
    part = w.shape[1] // 8
    places, at = [], 0
    for group in groups:
        places.append(tuple(range(at, at + len(group))))
        at += len(group)
    anywhere = pl.BlockSpec(memory_space=pl.ANY)
    return pl.pallas_call(
        functools.partial(loading, steps, places, kernel),
        out_shape=outs,
        in_specs=[pl.BlockSpec(memory_space=pltpu.SMEM), anywhere, anywhere],
        out_specs=[pl.BlockSpec(memory_space=pltpu.VMEM)] * len(outs),
        scratch_shapes=[
            pltpu.VMEM((rows, depth), x.dtype),
            pltpu.VMEM(w.shape, w.dtype),
            pltpu.VMEM((count, rows, part), jnp.float32),
            pltpu.SemaphoreType.DMA((CHUNKS,)),
            pltpu.SemaphoreType.DMA((CHUNKS,)),
        ],
        compiler_params=pltpu.CompilerParams(vmem_limit_bytes=52 * 2**20),
        cost_estimate=pl.CostEstimate(
            flops=2 * rows * depth * part * count,
            bytes_accessed=2 * depth * (rows + part * count),
            transcendentals=0,
        ),
    )(me, x, w)


def local_call(kernel, outs, *args, flops=0):
    return pl.pallas_call(
        kernel,
        out_shape=outs,
        compiler_params=pltpu.CompilerParams(vmem_limit_bytes=40 * 2**20),
        cost_estimate=pl.CostEstimate(flops=flops, bytes_accessed=2**20, transcendentals=0),
    )(*args)


def merge_kernel(own_a, next_a, far_a, own_b, next_b, far_b, qa, qb):
    half = own_a.shape[0] // 2
    total = own_a[...] + take_coded(next_a.at[0])
    total = jnp.concatenate([total[:half] + take_coded(far_a), total[half:]], axis=0)
    put_coded(qa, total)
    total = own_b[...] + take_coded(next_b.at[0])
    total = jnp.concatenate([total[:half], total[half:] + take_coded(far_b)], axis=0)
    put_coded(qb, total)


def selector_kernel(target_ref, out):
    places, rows = out.shape
    replicas = 32
    each = places // replicas
    target = target_ref[...]
    onehot = (lax.broadcasted_iota(jnp.int32, (replicas, rows), 0) == target).astype(jnp.float32)
    before = (
        lax.broadcasted_iota(jnp.int32, (rows, rows), 0)
        < lax.broadcasted_iota(jnp.int32, (rows, rows), 1)
    ).astype(jnp.bfloat16)
    ranks = jnp.dot(onehot.astype(jnp.bfloat16), before, preferred_element_type=jnp.float32)
    rank = jnp.sum(ranks * onehot, axis=0, keepdims=True).astype(jnp.int32)
    position = target * each + rank
    out[...] = (lax.broadcasted_iota(jnp.int32, (places, rows), 0) == position).astype(jnp.float32).astype(jnp.bfloat16)


def final_kernel(own, ra, rb, rc, rd, selector, out):
    keys = own[...] + take_coded(ra.at[1]) + take_coded(rb.at[1]) + take_coded(rc) + take_coded(rd)
    out[...] = jnp.dot(
        selector[...], keys.astype(jnp.bfloat16), preferred_element_type=jnp.float32
    ).astype(jnp.bfloat16)


def half_kernel(place, half, *refs):
    refs[-1][...] = half[...].reshape(refs[-1].shape)


def set_half(place, half, pair=None):
    lanes, rows, width = half.shape
    step = rows // 2
    args = (place, half) + (() if pair is None else (pair,))
    return pl.pallas_call(
        half_kernel,
        out_shape=jax.ShapeDtypeStruct((lanes, 2, rows, width), half.dtype),
        grid_spec=pltpu.PrefetchScalarGridSpec(
            num_scalar_prefetch=1,
            grid=(lanes, rows // step),
            in_specs=[pl.BlockSpec((1, step, width), lambda i, j, place: (i, j, 0))]
            + [pl.BlockSpec(memory_space=pl.ANY)] * (len(args) - 2),
            out_specs=pl.BlockSpec((1, 1, step, width), lambda i, j, place: (i, place[0], j, 0)),
        ),
        input_output_aliases={} if pair is None else {2: 0},
        compiler_params=pltpu.CompilerParams(vmem_limit_bytes=16 * 2**20),
        cost_estimate=pl.CostEstimate(flops=0, bytes_accessed=4 * half.size, transcendentals=0),
    )(*args)


def along_tp(value, step):
    size = lax.axis_size("tp")
    return lax.ppermute(value, "tp", [(i, (i + step) % size) for i in range(size)])


def local(master, moment, second, gradient, step_count, old_weights, branch_rows, assignment):
    rows, width = master.shape
    chips = lax.axis_size(CHIPS)
    size = lax.axis_size("tp")
    me = jnp.reshape(lax.axis_index("tp"), (1,)).astype(jnp.int32)
    count = branch_rows.shape[0]
    part = old_weights.shape[1] // size
    code = lambda *n: jax.ShapeDtypeStruct(n[:-1] + (n[-1] + TAIL, part), jnp.int16)
    full = jax.ShapeDtypeStruct((count, part), jnp.float32)
    new_master, new_moment, new_second, spread = updated(
        step_count, master, moment, second, gradient, chips
    )
    mine = lax.all_to_all(spread, CHIPS, split_axis=0, concat_axis=0, tiled=True)
    up, down, far_up, far_down, p2, p6, p0 = products(
        products_kernel, branch_rows, old_weights, me, ((3, 5), (4, 0), (2, 6), (1, 7)),
        [code(2, count)] * 2 + [code(count // 2)] * 2 + [full] * 3,
    )
    up, down = along_tp(up, 1), along_tp(down, -1)
    far_up, far_down = along_tp(far_up, 2), along_tp(far_down, -2)
    q2, q6 = local_call(merge_kernel, [code(count), code(count)], p2, up, far_up, p6, down, far_down)
    r2, r6 = along_tp(q2, 2), along_tp(q6, -2)
    replicas = lax.axis_size(PLANE)
    slots_each = 2 * count // replicas
    places = replicas * slots_each
    selector = local_call(
        selector_kernel, jax.ShapeDtypeStruct((places, count), jnp.bfloat16), assignment.reshape(1, count)
    )
    placed = local_call(
        final_kernel, jax.ShapeDtypeStruct((places, part), jnp.bfloat16), p0, up, down, r2, r6, selector
    )
    mine = lax.optimization_barrier((mine, placed))[0]
    placed = placed.reshape(replicas, slots_each, part)
    arrived = lax.all_to_all(placed, PLANE, split_axis=0, concat_axis=0, tiled=True)
    other = lax.ppermute(mine, "core", [(0, 1), (1, 0)])
    core = jnp.reshape(lax.axis_index("core"), (1,)).astype(jnp.int32)
    lanes = lax.axis_size("xlo")
    mine = mine.reshape(lanes, -1, width)
    other = other.reshape(lanes, -1, width)
    pair = set_half(core, mine)
    pair = set_half(1 - core, other, pair)
    pair, arrived = lax.optimization_barrier((pair, arrived))
    branch_keys = arrived.reshape(1, replicas, slots_each, part)
    rollout_weights = pair.reshape(2 * chips * rows, width)
    return (new_master, new_moment, new_second, rollout_weights, branch_keys)


def solution(mesh):
    size = mesh.shape
    mesh = Mesh(
        mesh.devices.reshape(2, 2, 4, 2, size["tp"]), ("xlo", "core", "y", "xhi", "tp")
    )
    shard = P(("tp",) + PLANE, None)
    return jax.shard_map(
        local,
        mesh=mesh,
        in_specs=(shard, shard, shard, shard, P(), P("tp", None), P(PLANE, "tp"), P(PLANE, None)),
        out_specs=(shard, shard, shard, P("tp", None), P(PLANE, None, None, "tp")),
        check_vma=False,
    )
```

```python
import functools

import jax
import jax.numpy as jnp
from jax import lax
from jax.experimental import pallas as pl
from jax.experimental.pallas import tpu as pltpu
from jax.sharding import Mesh
from jax.sharding import PartitionSpec as P

learn_rate = 0.05
decay_rate = 0.1

PLANE = ("xlo", "core", "y", "xhi")
CHIPS = ("xlo", "y", "xhi")
LEVELS = 32767.0
TAIL = 16
CHUNKS = 4
MOST_STEPS = 8


def coded(value):
    top = jnp.maximum(jnp.max(jnp.abs(value), axis=0, keepdims=True), 1.2e-38)
    power = jnp.ceil(jnp.log(top) * (256.0 / 0.6931471805599453) + 0.01)
    power = jnp.clip(power, -32256.0, 32256.0)
    scaled = value * jnp.exp2(power * (-1.0 / 256.0)) * LEVELS
    codes = jnp.clip(jnp.round(scaled), -LEVELS, LEVELS)
    tail = jnp.broadcast_to(power, (TAIL, value.shape[1]))
    return codes.astype(jnp.int32).astype(jnp.int16), tail.astype(jnp.int32).astype(jnp.int16)


def put_coded(ref, value):
    codes, tail = coded(value)
    rows = value.shape[0]
    ref[0:rows, :] = codes
    ref[rows : rows + TAIL, :] = tail


def take_coded(ref):
    rows = ref.shape[0] - TAIL
    power = ref[rows : rows + TAIL, :].astype(jnp.int32).astype(jnp.float32)[0:1, :]
    codes = ref[0:rows, :].astype(jnp.int32).astype(jnp.float32)
    return codes * (1.0 / LEVELS) * jnp.exp2(power * (1.0 / 256.0))


def adamw(steps, master, moment, second, gradient):
    first = other = jnp.ones(steps.shape, jnp.float32)
    for k in range(MOST_STEPS):
        first = jnp.where(steps > k, first * 0.9, first)
        other = jnp.where(steps > k, other * 0.95, other)
    first_part, second_part = 1.0 / (1.0 - first), 1.0 / (1.0 - other)
    m = 0.9 * moment + 0.1 * gradient
    v = 0.95 * second + 0.05 * gradient * gradient
    update = m * first_part / (jnp.sqrt(v * second_part) + 1e-08)
    return master - learn_rate * (update + decay_rate * master), m, v


def update_kernel(step_h, master_h, moment_h, second_h, gradient_h, *refs):
    count = len(refs) - 8
    outs, (step, master, moment, second, gradient, results, sems, out_sems) = refs[:count], refs[count:]
    sources = [step_h, moment_h, gradient_h, second_h, master_h]
    places = [step, moment, gradient, second, master]
    loads = [
        pltpu.make_async_copy(source, place, sems.at[k])
        for k, (source, place) in enumerate(zip(sources, places))
    ]
    for load in loads:
        load.start()
    for load in loads:
        load.wait()
    steps = jnp.broadcast_to(step[...], (1, master.shape[1]))
    values = adamw(steps, master[...], moment[...], second[...], gradient[...])
    if count == 1:
        results[0] = values[0].astype(results.dtype)
        pairs = [(results.at[0], outs[0].at[k]) for k in range(outs[0].shape[0])]
    else:
        for k, value in enumerate(values):
            results[k] = value
        pairs = [(results.at[k], out) for k, out in enumerate(outs)]
    stores = [
        pltpu.make_async_copy(source, place, out_sems.at[k])
        for k, (source, place) in enumerate(pairs)
    ]
    for store in stores:
        store.start()
    for store in stores:
        store.wait()


def updated(step_count, master, moment, second, gradient, chips=None):
    anywhere = pl.BlockSpec(memory_space=pl.ANY)
    shard = master.shape
    if chips is None:
        outs, kind, copies = [jax.ShapeDtypeStruct(shard, jnp.float32)] * 3, jnp.float32, 3
    else:
        outs, kind, copies = [jax.ShapeDtypeStruct((chips,) + shard, jnp.bfloat16)], jnp.bfloat16, chips
    return pl.pallas_call(
        update_kernel,
        out_shape=outs,
        in_specs=[anywhere] * 5,
        out_specs=[anywhere] * len(outs),
        scratch_shapes=[pltpu.VMEM((1, 1), jnp.int32)]
        + [pltpu.VMEM(shard, jnp.float32)] * 4
        + [
            pltpu.VMEM((len(outs),) + shard, kind),
            pltpu.SemaphoreType.DMA((5,)),
            pltpu.SemaphoreType.DMA((copies,)),
        ],
        compiler_params=pltpu.CompilerParams(vmem_limit_bytes=(60 if chips else 54) * 2**20),
        cost_estimate=pl.CostEstimate(
            flops=30 * master.size, bytes_accessed=28 * master.size, transcendentals=3 * master.size
        ),
    )(step_count.reshape(1, 1), master, moment, second, gradient)


def loading(steps, groups, kernel, me, x_h, w_h, *refs):
    x, w, totals, x_sems, w_sems = refs[-5:]
    part = totals.shape[2]
    blocks = [lax.rem(me[0] + step, len(steps)) * part for step in steps]
    depth = x.shape[1] // CHUNKS
    loads = []
    for c in range(CHUNKS):
        chunk = pl.ds(c * depth, depth)
        group = [
            pltpu.make_async_copy(x_h.at[:, chunk], x.at[:, chunk], x_sems.at[c]),
            pltpu.make_async_copy(w_h.at[chunk], w.at[chunk], w_sems.at[c]),
        ]
        loads.append(group)
        for load in group:
            load.start()
    for c in range(CHUNKS):
        chunk = slice(c * depth, (c + 1) * depth)
        for load in loads[c]:
            load.wait()
        for group in groups:
            columns = jnp.concatenate(
                [w[chunk, pl.ds(pl.multiple_of(blocks[k], part), part)] for k in group], axis=1
            )
            value = jnp.dot(x[:, chunk], columns, preferred_element_type=jnp.float32)
            for i, k in enumerate(group):
                share = value[:, i * part : (i + 1) * part]
                totals[k] = share if c == 0 else totals[k] + share
    kernel(totals, *refs[:-5])


def products_kernel(totals, up, down, far_up, far_down, next_up, next_down, two_up, two_down, own):
    half = totals.shape[1] // 2
    put_coded(up, totals[0])
    put_coded(down, totals[1])
    put_coded(far_up, totals[2, :half])
    put_coded(far_down, totals[2, half:])
    own[...] = totals[3]
    two_up[...] = totals[4]
    two_down[...] = totals[5]
    put_coded(next_up, totals[6])
    put_coded(next_down, totals[7])


def products(kernel, x, w, me, groups, outs):
    rows, depth = x.shape
    steps = [step for group in groups for step in group]
    count = len(steps)
    part = w.shape[1] // 8
    places, at = [], 0
    for group in groups:
        places.append(tuple(range(at, at + len(group))))
        at += len(group)
    anywhere = pl.BlockSpec(memory_space=pl.ANY)
    return pl.pallas_call(
        functools.partial(loading, steps, places, kernel),
        out_shape=outs,
        in_specs=[pl.BlockSpec(memory_space=pltpu.SMEM), anywhere, anywhere],
        out_specs=[pl.BlockSpec(memory_space=pltpu.VMEM)] * len(outs),
        scratch_shapes=[
            pltpu.VMEM((rows, depth), x.dtype),
            pltpu.VMEM(w.shape, w.dtype),
            pltpu.VMEM((count, rows, part), jnp.float32),
            pltpu.SemaphoreType.DMA((CHUNKS,)),
            pltpu.SemaphoreType.DMA((CHUNKS,)),
        ],
        compiler_params=pltpu.CompilerParams(vmem_limit_bytes=52 * 2**20),
        cost_estimate=pl.CostEstimate(
            flops=2 * rows * depth * part * count,
            bytes_accessed=2 * depth * (rows + part * count),
            transcendentals=0,
        ),
    )(me, x, w)


def local_call(kernel, outs, *args, flops=0):
    return pl.pallas_call(
        kernel,
        out_shape=outs,
        compiler_params=pltpu.CompilerParams(vmem_limit_bytes=40 * 2**20),
        cost_estimate=pl.CostEstimate(flops=flops, bytes_accessed=2**20, transcendentals=0),
    )(*args)


def merge_kernel(own_a, next_a, far_a, own_b, next_b, far_b, qa, qb):
    half = own_a.shape[0] // 2
    total = own_a[...] + take_coded(next_a)
    total = jnp.concatenate([total[:half] + take_coded(far_a), total[half:]], axis=0)
    put_coded(qa, total)
    total = own_b[...] + take_coded(next_b)
    total = jnp.concatenate([total[:half], total[half:] + take_coded(far_b)], axis=0)
    put_coded(qb, total)


def selector_kernel(target_ref, out):
    places, rows = out.shape
    replicas = 32
    each = places // replicas
    target = target_ref[...]
    onehot = (lax.broadcasted_iota(jnp.int32, (replicas, rows), 0) == target).astype(jnp.float32)
    before = (
        lax.broadcasted_iota(jnp.int32, (rows, rows), 0)
        < lax.broadcasted_iota(jnp.int32, (rows, rows), 1)
    ).astype(jnp.bfloat16)
    ranks = jnp.dot(onehot.astype(jnp.bfloat16), before, preferred_element_type=jnp.float32)
    rank = jnp.sum(ranks * onehot, axis=0, keepdims=True).astype(jnp.int32)
    position = target * each + rank
    out[...] = (lax.broadcasted_iota(jnp.int32, (places, rows), 0) == position).astype(jnp.float32).astype(jnp.bfloat16)


def final_kernel(own, ra, rb, rc, rd, selector, out):
    keys = own[...] + take_coded(ra) + take_coded(rb) + take_coded(rc) + take_coded(rd)
    out[...] = jnp.dot(
        selector[...], keys.astype(jnp.bfloat16), preferred_element_type=jnp.float32
    ).astype(jnp.bfloat16)


def half_kernel(place, half, *refs):
    refs[-1][...] = half[...].reshape(refs[-1].shape)


def set_half(place, half, pair=None):
    lanes, rows, width = half.shape
    step = rows // 2
    args = (place, half) + (() if pair is None else (pair,))
    return pl.pallas_call(
        half_kernel,
        out_shape=jax.ShapeDtypeStruct((lanes, 2, rows, width), half.dtype),
        grid_spec=pltpu.PrefetchScalarGridSpec(
            num_scalar_prefetch=1,
            grid=(lanes, rows // step),
            in_specs=[pl.BlockSpec((1, step, width), lambda i, j, place: (i, j, 0))]
            + [pl.BlockSpec(memory_space=pl.ANY)] * (len(args) - 2),
            out_specs=pl.BlockSpec((1, 1, step, width), lambda i, j, place: (i, place[0], j, 0)),
        ),
        input_output_aliases={} if pair is None else {2: 0},
        compiler_params=pltpu.CompilerParams(vmem_limit_bytes=16 * 2**20),
        cost_estimate=pl.CostEstimate(flops=0, bytes_accessed=4 * half.size, transcendentals=0),
    )(*args)


def along_tp(value, step):
    size = lax.axis_size("tp")
    return lax.ppermute(value, "tp", [(i, (i + step) % size) for i in range(size)])


def local(master, moment, second, gradient, step_count, old_weights, branch_rows, assignment):
    rows, width = master.shape
    chips = lax.axis_size(CHIPS)
    size = lax.axis_size("tp")
    me = jnp.reshape(lax.axis_index("tp"), (1,)).astype(jnp.int32)
    count = branch_rows.shape[0]
    part = old_weights.shape[1] // size
    code = lambda n: jax.ShapeDtypeStruct((n + TAIL, part), jnp.int16)
    full = jax.ShapeDtypeStruct((count, part), jnp.float32)
    (spread,) = updated(step_count, master, moment, second, gradient, chips)
    mine = lax.all_to_all(spread, CHIPS, split_axis=0, concat_axis=0, tiled=True)
    q3, q5, q4a, q4b, q1, q7, p2, p6, p0 = products(
        products_kernel, branch_rows, old_weights, me, ((3, 5), (4, 0), (2, 6), (1, 7)),
        [code(count)] * 2 + [code(count // 2)] * 2 + [code(count)] * 2 + [full] * 3,
    )
    r3, r5 = along_tp(q3, 1), along_tp(q5, -1)
    r4a, r4b = along_tp(q4a, 2), along_tp(q4b, -2)
    r1, r7 = along_tp(q1, 1), along_tp(q7, -1)
    q2, q6 = local_call(merge_kernel, [code(count), code(count)], p2, r3, r4a, p6, r5, r4b)
    r2, r6 = along_tp(q2, 2), along_tp(q6, -2)
    late = lax.optimization_barrier((master, q2, q6))[0]
    new_master, new_moment, new_second = updated(step_count, late, moment, second, gradient)
    p0 = lax.optimization_barrier((p0, new_master))[0]
    replicas = lax.axis_size(PLANE)
    slots_each = 2 * count // replicas
    places = replicas * slots_each
    selector = local_call(
        selector_kernel, jax.ShapeDtypeStruct((places, count), jnp.bfloat16), assignment.reshape(1, count)
    )
    placed = local_call(
        final_kernel, jax.ShapeDtypeStruct((places, part), jnp.bfloat16), p0, r1, r7, r2, r6, selector
    )
    mine = lax.optimization_barrier((mine, placed))[0]
    placed = placed.reshape(replicas, slots_each, part)
    arrived = lax.all_to_all(placed, PLANE, split_axis=0, concat_axis=0, tiled=True)
    other = lax.ppermute(mine, "core", [(0, 1), (1, 0)])
    core = jnp.reshape(lax.axis_index("core"), (1,)).astype(jnp.int32)
    lanes = lax.axis_size("xlo")
    mine = mine.reshape(lanes, -1, width)
    other = other.reshape(lanes, -1, width)
    pair = set_half(core, mine)
    pair = set_half(1 - core, other, pair)
    pair, arrived = lax.optimization_barrier((pair, arrived))
    branch_keys = arrived.reshape(1, replicas, slots_each, part)
    rollout_weights = pair.reshape(2 * chips * rows, width)
    return (new_master, new_moment, new_second, rollout_weights, branch_keys)


def solution(mesh):
    size = mesh.shape
    mesh = Mesh(
        mesh.devices.reshape(2, 2, 4, 2, size["tp"]), ("xlo", "core", "y", "xhi", "tp")
    )
    shard = P(("tp",) + PLANE, None)
    return jax.shard_map(
        local,
        mesh=mesh,
        in_specs=(shard, shard, shard, shard, P(), P("tp", None), P(PLANE, "tp"), P(PLANE, None)),
        out_specs=(shard, shard, shard, P("tp", None), P(PLANE, None, None, "tp")),
        check_vma=False,
    )
```

```python
import functools

import jax
import jax.numpy as jnp
from jax import lax
from jax.experimental import pallas as pl
from jax.experimental.pallas import tpu as pltpu
from jax.sharding import Mesh
from jax.sharding import PartitionSpec as P

learn_rate = 0.05
decay_rate = 0.1

PLANE = ("xlo", "core", "y", "xhi")
CHIPS = ("xlo", "y", "xhi")
LEVELS = 32767.0
TAIL = 16
CHUNKS = 4
MOST_STEPS = 8


def coded(value):
    top = jnp.maximum(jnp.max(jnp.abs(value), axis=0, keepdims=True), 1.2e-38)
    power = jnp.ceil(jnp.log(top) * (256.0 / 0.6931471805599453) + 0.01)
    power = jnp.clip(power, -32256.0, 32256.0)
    scaled = value * jnp.exp2(power * (-1.0 / 256.0)) * LEVELS
    codes = jnp.clip(jnp.round(scaled), -LEVELS, LEVELS)
    tail = jnp.broadcast_to(power, (TAIL, value.shape[1]))
    return codes.astype(jnp.int32).astype(jnp.int16), tail.astype(jnp.int32).astype(jnp.int16)


def put_coded(ref, value):
    codes, tail = coded(value)
    rows = value.shape[0]
    ref[0:rows, :] = codes
    ref[rows : rows + TAIL, :] = tail


def take_coded(ref):
    rows = ref.shape[0] - TAIL
    power = ref[rows : rows + TAIL, :].astype(jnp.int32).astype(jnp.float32)[0:1, :]
    codes = ref[0:rows, :].astype(jnp.int32).astype(jnp.float32)
    return codes * (1.0 / LEVELS) * jnp.exp2(power * (1.0 / 256.0))


def adamw(steps, master, moment, second, gradient):
    first = other = jnp.ones(steps.shape, jnp.float32)
    for k in range(MOST_STEPS):
        first = jnp.where(steps > k, first * 0.9, first)
        other = jnp.where(steps > k, other * 0.95, other)
    first_part, second_part = 1.0 / (1.0 - first), 1.0 / (1.0 - other)
    m = 0.9 * moment + 0.1 * gradient
    v = 0.95 * second + 0.05 * gradient * gradient
    update = m * first_part / (jnp.sqrt(v * second_part) + 1e-08)
    return master - learn_rate * (update + decay_rate * master), m, v


def update_kernel(step_h, master_h, moment_h, second_h, gradient_h, *refs):
    count = len(refs) - 8
    outs, (step, master, moment, second, gradient, results, sems, out_sems) = refs[:count], refs[count:]
    sources = [step_h, moment_h, gradient_h, second_h, master_h]
    places = [step, moment, gradient, second, master]
    loads = [
        pltpu.make_async_copy(source, place, sems.at[k])
        for k, (source, place) in enumerate(zip(sources, places))
    ]
    for load in loads:
        load.start()
    for load in loads:
        load.wait()
    steps = jnp.broadcast_to(step[...], (1, master.shape[1]))
    values = adamw(steps, master[...], moment[...], second[...], gradient[...])
    if count == 1:
        results[0] = values[0].astype(results.dtype)
        pairs = [(results.at[0], outs[0].at[k]) for k in range(outs[0].shape[0])]
    else:
        for k, value in enumerate(values):
            results[k] = value
        pairs = [(results.at[k], out) for k, out in enumerate(outs)]
    stores = [
        pltpu.make_async_copy(source, place, out_sems.at[k])
        for k, (source, place) in enumerate(pairs)
    ]
    for store in stores:
        store.start()
    for store in stores:
        store.wait()


def updated(step_count, master, moment, second, gradient, chips=None):
    anywhere = pl.BlockSpec(memory_space=pl.ANY)
    shard = master.shape
    if chips is None:
        outs, kind, copies = [jax.ShapeDtypeStruct(shard, jnp.float32)] * 3, jnp.float32, 3
    else:
        outs, kind, copies = [jax.ShapeDtypeStruct((chips,) + shard, jnp.bfloat16)], jnp.bfloat16, chips
    return pl.pallas_call(
        update_kernel,
        out_shape=outs,
        in_specs=[anywhere] * 5,
        out_specs=[anywhere] * len(outs),
        scratch_shapes=[pltpu.VMEM((1, 1), jnp.int32)]
        + [pltpu.VMEM(shard, jnp.float32)] * 4
        + [
            pltpu.VMEM((len(outs),) + shard, kind),
            pltpu.SemaphoreType.DMA((5,)),
            pltpu.SemaphoreType.DMA((copies,)),
        ],
        compiler_params=pltpu.CompilerParams(vmem_limit_bytes=(60 if chips else 54) * 2**20),
        cost_estimate=pl.CostEstimate(
            flops=30 * master.size, bytes_accessed=28 * master.size, transcendentals=3 * master.size
        ),
    )(step_count.reshape(1, 1), master, moment, second, gradient)


def loading(steps, groups, kernel, me, x_h, w_h, *refs):
    x, w, totals, x_sems, w_sems = refs[-5:]
    part = totals.shape[2]
    blocks = [lax.rem(me[0] + step, len(steps)) * part for step in steps]
    depth = x.shape[1] // CHUNKS
    loads = []
    for c in range(CHUNKS):
        chunk = pl.ds(c * depth, depth)
        group = [
            pltpu.make_async_copy(x_h.at[:, chunk], x.at[:, chunk], x_sems.at[c]),
            pltpu.make_async_copy(w_h.at[chunk], w.at[chunk], w_sems.at[c]),
        ]
        loads.append(group)
        for load in group:
            load.start()
    for c in range(CHUNKS):
        chunk = slice(c * depth, (c + 1) * depth)
        for load in loads[c]:
            load.wait()
        for group in groups:
            columns = jnp.concatenate(
                [w[chunk, pl.ds(pl.multiple_of(blocks[k], part), part)] for k in group], axis=1
            )
            value = jnp.dot(x[:, chunk], columns, preferred_element_type=jnp.float32)
            for i, k in enumerate(group):
                share = value[:, i * part : (i + 1) * part]
                totals[k] = share if c == 0 else totals[k] + share
    kernel(totals, *refs[:-5])


def products_kernel(totals, up, down, far_up, far_down, next_up, next_down, two_up, two_down, own):
    half = totals.shape[1] // 2
    put_coded(up, totals[0])
    put_coded(down, totals[1])
    put_coded(far_up, totals[2, :half])
    put_coded(far_down, totals[2, half:])
    own[...] = totals[3]
    two_up[...] = totals[4]
    two_down[...] = totals[5]
    put_coded(next_up, totals[6])
    put_coded(next_down, totals[7])


def products(kernel, x, w, me, groups, outs):
    rows, depth = x.shape
    steps = [step for group in groups for step in group]
    count = len(steps)
    part = w.shape[1] // 8
    places, at = [], 0
    for group in groups:
        places.append(tuple(range(at, at + len(group))))
        at += len(group)
    anywhere = pl.BlockSpec(memory_space=pl.ANY)
    return pl.pallas_call(
        functools.partial(loading, steps, places, kernel),
        out_shape=outs,
        in_specs=[pl.BlockSpec(memory_space=pltpu.SMEM), anywhere, anywhere],
        out_specs=[pl.BlockSpec(memory_space=pltpu.VMEM)] * len(outs),
        scratch_shapes=[
            pltpu.VMEM((rows, depth), x.dtype),
            pltpu.VMEM(w.shape, w.dtype),
            pltpu.VMEM((count, rows, part), jnp.float32),
            pltpu.SemaphoreType.DMA((CHUNKS,)),
            pltpu.SemaphoreType.DMA((CHUNKS,)),
        ],
        compiler_params=pltpu.CompilerParams(vmem_limit_bytes=52 * 2**20),
        cost_estimate=pl.CostEstimate(
            flops=2 * rows * depth * part * count,
            bytes_accessed=2 * depth * (rows + part * count),
            transcendentals=0,
        ),
    )(me, x, w)


def local_call(kernel, outs, *args, flops=0):
    return pl.pallas_call(
        kernel,
        out_shape=outs,
        compiler_params=pltpu.CompilerParams(vmem_limit_bytes=40 * 2**20),
        cost_estimate=pl.CostEstimate(flops=flops, bytes_accessed=2**20, transcendentals=0),
    )(*args)


def merge_kernel(own_a, next_a, far_a, own_b, next_b, far_b, qa, qb):
    half = own_a.shape[0] // 2
    total = own_a[...] + take_coded(next_a)
    total = jnp.concatenate([total[:half] + take_coded(far_a), total[half:]], axis=0)
    put_coded(qa, total)
    total = own_b[...] + take_coded(next_b)
    total = jnp.concatenate([total[:half], total[half:] + take_coded(far_b)], axis=0)
    put_coded(qb, total)


def selector_kernel(target_ref, out):
    places, rows = out.shape
    replicas = 32
    each = places // replicas
    target = target_ref[...]
    onehot = (lax.broadcasted_iota(jnp.int32, (replicas, rows), 0) == target).astype(jnp.float32)
    before = (
        lax.broadcasted_iota(jnp.int32, (rows, rows), 0)
        < lax.broadcasted_iota(jnp.int32, (rows, rows), 1)
    ).astype(jnp.bfloat16)
    ranks = jnp.dot(onehot.astype(jnp.bfloat16), before, preferred_element_type=jnp.float32)
    rank = jnp.sum(ranks * onehot, axis=0, keepdims=True).astype(jnp.int32)
    position = target * each + rank
    out[...] = (lax.broadcasted_iota(jnp.int32, (places, rows), 0) == position).astype(jnp.float32).astype(jnp.bfloat16)


def final_kernel(own, ra, rb, rc, rd, selector, out):
    keys = own[...] + take_coded(ra) + take_coded(rb) + take_coded(rc) + take_coded(rd)
    out[...] = jnp.dot(
        selector[...], keys.astype(jnp.bfloat16), preferred_element_type=jnp.float32
    ).astype(jnp.bfloat16)


def half_kernel(place, half, *refs):
    refs[-1][...] = half[...].reshape(refs[-1].shape)


def set_half(place, half, pair=None):
    lanes, rows, width = half.shape
    step = rows // 2
    args = (place, half) + (() if pair is None else (pair,))
    return pl.pallas_call(
        half_kernel,
        out_shape=jax.ShapeDtypeStruct((lanes, 2, rows, width), half.dtype),
        grid_spec=pltpu.PrefetchScalarGridSpec(
            num_scalar_prefetch=1,
            grid=(lanes, rows // step),
            in_specs=[pl.BlockSpec((1, step, width), lambda i, j, place: (i, j, 0))]
            + [pl.BlockSpec(memory_space=pl.ANY)] * (len(args) - 2),
            out_specs=pl.BlockSpec((1, 1, step, width), lambda i, j, place: (i, place[0], j, 0)),
        ),
        input_output_aliases={} if pair is None else {2: 0},
        compiler_params=pltpu.CompilerParams(vmem_limit_bytes=16 * 2**20),
        cost_estimate=pl.CostEstimate(flops=0, bytes_accessed=4 * half.size, transcendentals=0),
    )(*args)


def along_tp(value, step):
    size = lax.axis_size("tp")
    return lax.ppermute(value, "tp", [(i, (i + step) % size) for i in range(size)])


def local(master, moment, second, gradient, step_count, old_weights, branch_rows, assignment):
    rows, width = master.shape
    chips = lax.axis_size(CHIPS)
    size = lax.axis_size("tp")
    me = jnp.reshape(lax.axis_index("tp"), (1,)).astype(jnp.int32)
    count = branch_rows.shape[0]
    part = old_weights.shape[1] // size
    code = lambda n: jax.ShapeDtypeStruct((n + TAIL, part), jnp.int16)
    full = jax.ShapeDtypeStruct((count, part), jnp.float32)
    (spread,) = updated(step_count, master, moment, second, gradient, chips)
    mine = lax.all_to_all(spread, CHIPS, split_axis=0, concat_axis=0, tiled=True)
    q3, q5, q4a, q4b, q1, q7, p2, p6, p0 = products(
        products_kernel, branch_rows, old_weights, me, ((3, 5), (4, 0), (2, 6), (1, 7)),
        [code(count)] * 2 + [code(count // 2)] * 2 + [code(count)] * 2 + [full] * 3,
    )
    r3, r5 = along_tp(q3, 1), along_tp(q5, -1)
    r4a, r4b = along_tp(q4a, 2), along_tp(q4b, -2)
    r1 = along_tp(q1, 1)
    q2, q6 = local_call(merge_kernel, [code(count), code(count)], p2, r3, r4a, p6, r5, r4b)
    r2, r6 = along_tp(q2, 2), along_tp(q6, -2)
    q7 = lax.optimization_barrier((q7, q2))[0]
    r7 = along_tp(q7, -1)
    late = lax.optimization_barrier((master, q2, q6))[0]
    new_master, new_moment, new_second = updated(step_count, late, moment, second, gradient)
    p0 = lax.optimization_barrier((p0, new_master))[0]
    replicas = lax.axis_size(PLANE)
    slots_each = 2 * count // replicas
    places = replicas * slots_each
    selector = local_call(
        selector_kernel, jax.ShapeDtypeStruct((places, count), jnp.bfloat16), assignment.reshape(1, count)
    )
    placed = local_call(
        final_kernel, jax.ShapeDtypeStruct((places, part), jnp.bfloat16), p0, r1, r7, r2, r6, selector
    )
    mine = lax.optimization_barrier((mine, placed))[0]
    placed = placed.reshape(replicas, slots_each, part)
    arrived = lax.all_to_all(placed, PLANE, split_axis=0, concat_axis=0, tiled=True)
    other = lax.ppermute(mine, "core", [(0, 1), (1, 0)])
    core = jnp.reshape(lax.axis_index("core"), (1,)).astype(jnp.int32)
    lanes = lax.axis_size("xlo")
    mine = mine.reshape(lanes, -1, width)
    other = other.reshape(lanes, -1, width)
    pair = set_half(core, mine)
    pair = set_half(1 - core, other, pair)
    pair, arrived = lax.optimization_barrier((pair, arrived))
    branch_keys = arrived.reshape(1, replicas, slots_each, part)
    rollout_weights = pair.reshape(2 * chips * rows, width)
    return (new_master, new_moment, new_second, rollout_weights, branch_keys)


def solution(mesh):
    size = mesh.shape
    mesh = Mesh(
        mesh.devices.reshape(2, 2, 4, 2, size["tp"]), ("xlo", "core", "y", "xhi", "tp")
    )
    shard = P(("tp",) + PLANE, None)
    return jax.shard_map(
        local,
        mesh=mesh,
        in_specs=(shard, shard, shard, shard, P(), P("tp", None), P(PLANE, "tp"), P(PLANE, None)),
        out_specs=(shard, shard, shard, P("tp", None), P(PLANE, None, None, "tp")),
        check_vma=False,
    )
```

```python
import functools

import jax
import jax.numpy as jnp
from jax import lax
from jax.experimental import pallas as pl
from jax.experimental.pallas import tpu as pltpu
from jax.sharding import Mesh
from jax.sharding import PartitionSpec as P

learn_rate = 0.05
decay_rate = 0.1

PLANE = ("xlo", "core", "y", "xhi")
CHIPS = ("xlo", "y", "xhi")
LEVELS = 32767.0
TAIL = 16
CHUNKS = 4
MOST_STEPS = 8


def coded(value):
    top = jnp.maximum(jnp.max(jnp.abs(value), axis=0, keepdims=True), 1.2e-38)
    power = jnp.ceil(jnp.log(top) * (256.0 / 0.6931471805599453) + 0.01)
    power = jnp.clip(power, -32256.0, 32256.0)
    scaled = value * jnp.exp2(power * (-1.0 / 256.0)) * LEVELS
    codes = jnp.clip(jnp.round(scaled), -LEVELS, LEVELS)
    tail = jnp.broadcast_to(power, (TAIL, value.shape[1]))
    return codes.astype(jnp.int32).astype(jnp.int16), tail.astype(jnp.int32).astype(jnp.int16)


def put_coded(ref, value):
    codes, tail = coded(value)
    rows = value.shape[0]
    ref[0:rows, :] = codes
    ref[rows : rows + TAIL, :] = tail


def take_coded(ref):
    rows = ref.shape[0] - TAIL
    power = ref[rows : rows + TAIL, :].astype(jnp.int32).astype(jnp.float32)[0:1, :]
    codes = ref[0:rows, :].astype(jnp.int32).astype(jnp.float32)
    return codes * (1.0 / LEVELS) * jnp.exp2(power * (1.0 / 256.0))


def adamw(steps, master, moment, second, gradient):
    first = other = jnp.ones(steps.shape, jnp.float32)
    for k in range(MOST_STEPS):
        first = jnp.where(steps > k, first * 0.9, first)
        other = jnp.where(steps > k, other * 0.95, other)
    first_part, second_part = 1.0 / (1.0 - first), 1.0 / (1.0 - other)
    m = 0.9 * moment + 0.1 * gradient
    v = 0.95 * second + 0.05 * gradient * gradient
    update = m * first_part / (jnp.sqrt(v * second_part) + 1e-08)
    return master - learn_rate * (update + decay_rate * master), m, v


def update_kernel(step_h, master_h, moment_h, second_h, gradient_h, *refs):
    count = len(refs) - 8
    outs, (step, master, moment, second, gradient, results, sems, out_sems) = refs[:count], refs[count:]
    sources = [step_h, moment_h, gradient_h, second_h, master_h]
    places = [step, moment, gradient, second, master]
    loads = [
        pltpu.make_async_copy(source, place, sems.at[k])
        for k, (source, place) in enumerate(zip(sources, places))
    ]
    for load in loads:
        load.start()
    for load in loads:
        load.wait()
    steps = jnp.broadcast_to(step[...], (1, master.shape[1]))
    values = adamw(steps, master[...], moment[...], second[...], gradient[...])
    if count == 1:
        results[0] = values[0].astype(results.dtype)
        pairs = [(results.at[0], outs[0].at[k]) for k in range(outs[0].shape[0])]
    else:
        for k, value in enumerate(values):
            results[k] = value
        pairs = [(results.at[k], out) for k, out in enumerate(outs)]
    stores = [
        pltpu.make_async_copy(source, place, out_sems.at[k])
        for k, (source, place) in enumerate(pairs)
    ]
    for store in stores:
        store.start()
    for store in stores:
        store.wait()


def updated(step_count, master, moment, second, gradient, chips=None):
    anywhere = pl.BlockSpec(memory_space=pl.ANY)
    shard = master.shape
    if chips is None:
        outs, kind, copies = [jax.ShapeDtypeStruct(shard, jnp.float32)] * 3, jnp.float32, 3
    else:
        outs, kind, copies = [jax.ShapeDtypeStruct((chips,) + shard, jnp.bfloat16)], jnp.bfloat16, chips
    return pl.pallas_call(
        update_kernel,
        out_shape=outs,
        in_specs=[anywhere] * 5,
        out_specs=[anywhere] * len(outs),
        scratch_shapes=[pltpu.VMEM((1, 1), jnp.int32)]
        + [pltpu.VMEM(shard, jnp.float32)] * 4
        + [
            pltpu.VMEM((len(outs),) + shard, kind),
            pltpu.SemaphoreType.DMA((5,)),
            pltpu.SemaphoreType.DMA((copies,)),
        ],
        compiler_params=pltpu.CompilerParams(vmem_limit_bytes=(60 if chips else 54) * 2**20),
        cost_estimate=pl.CostEstimate(
            flops=30 * master.size, bytes_accessed=28 * master.size, transcendentals=3 * master.size
        ),
    )(step_count.reshape(1, 1), master, moment, second, gradient)


def loading(steps, groups, kernel, me, x_h, w_h, *refs):
    x, w, totals, x_sems, w_sems = refs[-5:]
    part = totals.shape[2]
    blocks = [lax.rem(me[0] + step, len(steps)) * part for step in steps]
    depth = x.shape[1] // CHUNKS
    loads = []
    for c in range(CHUNKS):
        chunk = pl.ds(c * depth, depth)
        group = [
            pltpu.make_async_copy(x_h.at[:, chunk], x.at[:, chunk], x_sems.at[c]),
            pltpu.make_async_copy(w_h.at[chunk], w.at[chunk], w_sems.at[c]),
        ]
        loads.append(group)
        for load in group:
            load.start()
    for c in range(CHUNKS):
        chunk = slice(c * depth, (c + 1) * depth)
        for load in loads[c]:
            load.wait()
        for group in groups:
            columns = jnp.concatenate(
                [w[chunk, pl.ds(pl.multiple_of(blocks[k], part), part)] for k in group], axis=1
            )
            value = jnp.dot(x[:, chunk], columns, preferred_element_type=jnp.float32)
            for i, k in enumerate(group):
                share = value[:, i * part : (i + 1) * part]
                totals[k] = share if c == 0 else totals[k] + share
    kernel(totals, *refs[:-5])


def products_kernel(totals, up, down, far_up, far_down, next_up, next_down, two_up, two_down, own):
    half = totals.shape[1] // 2
    put_coded(up, totals[0])
    put_coded(down, totals[1])
    put_coded(far_up, totals[2, :half])
    put_coded(far_down, totals[2, half:])
    own[...] = totals[3]
    two_up[...] = totals[4]
    two_down[...] = totals[5]
    put_coded(next_up, totals[6])
    put_coded(next_down, totals[7])


def products(kernel, x, w, me, groups, outs):
    rows, depth = x.shape
    steps = [step for group in groups for step in group]
    count = len(steps)
    part = w.shape[1] // 8
    places, at = [], 0
    for group in groups:
        places.append(tuple(range(at, at + len(group))))
        at += len(group)
    anywhere = pl.BlockSpec(memory_space=pl.ANY)
    return pl.pallas_call(
        functools.partial(loading, steps, places, kernel),
        out_shape=outs,
        in_specs=[pl.BlockSpec(memory_space=pltpu.SMEM), anywhere, anywhere],
        out_specs=[pl.BlockSpec(memory_space=pltpu.VMEM)] * len(outs),
        scratch_shapes=[
            pltpu.VMEM((rows, depth), x.dtype),
            pltpu.VMEM(w.shape, w.dtype),
            pltpu.VMEM((count, rows, part), jnp.float32),
            pltpu.SemaphoreType.DMA((CHUNKS,)),
            pltpu.SemaphoreType.DMA((CHUNKS,)),
        ],
        compiler_params=pltpu.CompilerParams(vmem_limit_bytes=52 * 2**20),
        cost_estimate=pl.CostEstimate(
            flops=2 * rows * depth * part * count,
            bytes_accessed=2 * depth * (rows + part * count),
            transcendentals=0,
        ),
    )(me, x, w)


def local_call(kernel, outs, *args, flops=0):
    return pl.pallas_call(
        kernel,
        out_shape=outs,
        compiler_params=pltpu.CompilerParams(vmem_limit_bytes=40 * 2**20),
        cost_estimate=pl.CostEstimate(flops=flops, bytes_accessed=2**20, transcendentals=0),
    )(*args)


def merge_kernel(own_a, next_a, far_a, own_b, next_b, far_b, qa, qb):
    half = own_a.shape[0] // 2
    total = own_a[...] + take_coded(next_a)
    total = jnp.concatenate([total[:half] + take_coded(far_a), total[half:]], axis=0)
    put_coded(qa, total)
    total = own_b[...] + take_coded(next_b)
    total = jnp.concatenate([total[:half], total[half:] + take_coded(far_b)], axis=0)
    put_coded(qb, total)


def selector_kernel(target_ref, out):
    places, rows = out.shape
    replicas = 32
    each = places // replicas
    target = target_ref[...]
    onehot = (lax.broadcasted_iota(jnp.int32, (replicas, rows), 0) == target).astype(jnp.float32)
    before = (
        lax.broadcasted_iota(jnp.int32, (rows, rows), 0)
        < lax.broadcasted_iota(jnp.int32, (rows, rows), 1)
    ).astype(jnp.bfloat16)
    ranks = jnp.dot(onehot.astype(jnp.bfloat16), before, preferred_element_type=jnp.float32)
    rank = jnp.sum(ranks * onehot, axis=0, keepdims=True).astype(jnp.int32)
    position = target * each + rank
    out[...] = (lax.broadcasted_iota(jnp.int32, (places, rows), 0) == position).astype(jnp.float32).astype(jnp.bfloat16)


def final_kernel(own, ra, rb, rc, rd, selector, out):
    keys = own[...] + take_coded(ra) + take_coded(rb) + take_coded(rc) + take_coded(rd)
    out[...] = jnp.dot(
        selector[...], keys.astype(jnp.bfloat16), preferred_element_type=jnp.float32
    ).astype(jnp.bfloat16)


def half_kernel(place, half, *refs):
    refs[-1][...] = half[...].reshape(refs[-1].shape)


def set_half(place, half, pair=None):
    lanes, rows, width = half.shape
    step = rows // 2
    args = (place, half) + (() if pair is None else (pair,))
    return pl.pallas_call(
        half_kernel,
        out_shape=jax.ShapeDtypeStruct((lanes, 2, rows, width), half.dtype),
        grid_spec=pltpu.PrefetchScalarGridSpec(
            num_scalar_prefetch=1,
            grid=(lanes, rows // step),
            in_specs=[pl.BlockSpec((1, step, width), lambda i, j, place: (i, j, 0))]
            + [pl.BlockSpec(memory_space=pl.ANY)] * (len(args) - 2),
            out_specs=pl.BlockSpec((1, 1, step, width), lambda i, j, place: (i, place[0], j, 0)),
        ),
        input_output_aliases={} if pair is None else {2: 0},
        compiler_params=pltpu.CompilerParams(vmem_limit_bytes=16 * 2**20),
        cost_estimate=pl.CostEstimate(flops=0, bytes_accessed=4 * half.size, transcendentals=0),
    )(*args)


def along_tp(value, step):
    size = lax.axis_size("tp")
    return lax.ppermute(value, "tp", [(i, (i + step) % size) for i in range(size)])


def local(master, moment, second, gradient, step_count, old_weights, branch_rows, assignment):
    rows, width = master.shape
    chips = lax.axis_size(CHIPS)
    size = lax.axis_size("tp")
    me = jnp.reshape(lax.axis_index("tp"), (1,)).astype(jnp.int32)
    count = branch_rows.shape[0]
    part = old_weights.shape[1] // size
    code = lambda n: jax.ShapeDtypeStruct((n + TAIL, part), jnp.int16)
    full = jax.ShapeDtypeStruct((count, part), jnp.float32)
    (spread,) = updated(step_count, master, moment, second, gradient, chips)
    mine = lax.all_to_all(spread, CHIPS, split_axis=0, concat_axis=0, tiled=True)
    q3, q5, q4a, q4b, q1, q7, p2, p6, p0 = products(
        products_kernel, branch_rows, old_weights, me, ((3, 5), (4, 0), (2, 6), (1, 7)),
        [code(count)] * 2 + [code(count // 2)] * 2 + [code(count)] * 2 + [full] * 3,
    )
    r3, r5 = along_tp(q3, 1), along_tp(q5, -1)
    r4a, r4b = along_tp(q4a, 2), along_tp(q4b, -2)
    q2, q6 = local_call(merge_kernel, [code(count), code(count)], p2, r3, r4a, p6, r5, r4b)
    r2, r6 = along_tp(q2, 2), along_tp(q6, -2)
    q1, q7, _ = lax.optimization_barrier((q1, q7, q2))
    r1, r7 = along_tp(q1, 1), along_tp(q7, -1)
    late = lax.optimization_barrier((master, q2, q6))[0]
    new_master, new_moment, new_second = updated(step_count, late, moment, second, gradient)
    p0 = lax.optimization_barrier((p0, new_master))[0]
    replicas = lax.axis_size(PLANE)
    slots_each = 2 * count // replicas
    places = replicas * slots_each
    selector = local_call(
        selector_kernel, jax.ShapeDtypeStruct((places, count), jnp.bfloat16), assignment.reshape(1, count)
    )
    placed = local_call(
        final_kernel, jax.ShapeDtypeStruct((places, part), jnp.bfloat16), p0, r1, r7, r2, r6, selector
    )
    mine = lax.optimization_barrier((mine, placed))[0]
    placed = placed.reshape(replicas, slots_each, part)
    arrived = lax.all_to_all(placed, PLANE, split_axis=0, concat_axis=0, tiled=True)
    other = lax.ppermute(mine, "core", [(0, 1), (1, 0)])
    core = jnp.reshape(lax.axis_index("core"), (1,)).astype(jnp.int32)
    lanes = lax.axis_size("xlo")
    mine = mine.reshape(lanes, -1, width)
    other = other.reshape(lanes, -1, width)
    pair = set_half(core, mine)
    pair = set_half(1 - core, other, pair)
    pair, arrived = lax.optimization_barrier((pair, arrived))
    branch_keys = arrived.reshape(1, replicas, slots_each, part)
    rollout_weights = pair.reshape(2 * chips * rows, width)
    return (new_master, new_moment, new_second, rollout_weights, branch_keys)


def solution(mesh):
    size = mesh.shape
    mesh = Mesh(
        mesh.devices.reshape(2, 2, 4, 2, size["tp"]), ("xlo", "core", "y", "xhi", "tp")
    )
    shard = P(("tp",) + PLANE, None)
    return jax.shard_map(
        local,
        mesh=mesh,
        in_specs=(shard, shard, shard, shard, P(), P("tp", None), P(PLANE, "tp"), P(PLANE, None)),
        out_specs=(shard, shard, shard, P("tp", None), P(PLANE, None, None, "tp")),
        check_vma=False,
    )
```
